32 devices in a mesh: row: 4 (over y, x), col: 8 (over z, core).
Axes of the slice: x: 2, y: 2, z: 4, core: 2. Of those that a mesh axis runs over, the one named last changes fastest.
Arguments:
- features: bfloat16 [8, 512, 768], P(None, 'row', 'col'), may hold values from -6 to 6
- lengthscale: float32 [768], replicated, may hold values from 8 to 200
- noise: float32 [8, 512], P(None, 'row'), may hold values from 0.05 to 0.5
Outputs:
- panel: float32 [8, 512, 128], P(None, 'row')
- trailing: float32 [8, 512, 4, 1024], P(None, 'row', None, 'col')
The draws below stay inside these ranges and needn't reach their ends.
All inputs are finite; a program needn't handle non-finite values.
Results may differ from the reference program's by a relative error of at most 0.005.
Values may be sent and summed in bfloat16 or wider, within the bound.
No kernel may reach another device: no remote copies, remote signals or barrier semaphores. Data moves between devices by JAX's collectives and lax.ppermute only.
A program may use at most 64 MiB of HBM per device.

```python
import math
import jax
import jax.numpy as jnp
from jax import lax

D = 768
B = 128
TR = 8
N_ROW = 4
N_COL = 8


def block_levels(own_key, shape, cuts, least, high):
    level, own = 1.0, jax.random.fold_in(own_key, 6)
    for dim, shards_of in cuts:
        heights = jnp.exp(jax.random.uniform(jax.random.fold_in(own, dim), (shards_of,), jnp.float32, least / len(cuts), high / len(cuts)))
        level = level * jnp.repeat(heights, shape[dim] // shards_of).reshape([-1 if axis == dim else 1 for axis in range(len(shape))])
    return level


def scatter_about(own_key, dims, scale, most, shards=(), dtype=jnp.bfloat16):
    entries = jax.random.normal(own_key, dims, jnp.float32) * scale
    if len(shards) > 0:
        entries = block_levels(own_key, dims, shards, -0.22, 0.18) * entries
    return jnp.clip(entries, min=-most, max=most).astype(dtype)


def setup_inputs(seed: int = 0) -> dict:
    splits = jax.random.split(jax.random.key(seed), 4)
    return {
        "features": scatter_about(splits[0], (TR, N_ROW * B, D), 1.0, 6.0, ((1, 4), (2, 8))),
        "lengthscale": jnp.clip(jnp.exp(jax.random.uniform(splits[1], (D,), jnp.float32, math.log(8.0), math.log(200.0))), 8.0, 200.0),
        "noise": jnp.clip(jnp.exp(math.log(0.5) - 2.3025851 * jax.random.uniform(splits[2], (TR, N_ROW * B), jnp.float32) ** block_levels(splits[2], (TR, N_ROW * B), ((1, 4),), -0.2, 0.2)), 0.05, 0.5),
    }


def reference(features, lengthscale, noise):
    npts = features.shape[0] * features.shape[1]
    scaled = features.reshape(npts, features.shape[2]).astype(jnp.float32) / lengthscale[None, :]
    sq = jnp.sum(scaled * scaled, axis=1)
    gram = jnp.dot(scaled, scaled.T, precision=lax.Precision.HIGHEST)
    kern = jnp.exp(-0.5 * (sq[:, None] + sq[None, :] - 2.0 * gram))
    index = jnp.arange(npts)
    kern = kern.at[index, index].add(noise.reshape(npts))
    width = B
    factor = jnp.linalg.cholesky(kern[:width, :width])
    panel = jax.scipy.linalg.solve_triangular(factor, kern[:, :width].T, lower=True).T
    trailing = kern - jnp.dot(panel, panel.T, precision=lax.Precision.HIGHEST)
    rows = features.shape[1]
    tiles_col = npts // (N_COL * width)
    return (panel.reshape(features.shape[0], rows, width), trailing.reshape(features.shape[0], rows, tiles_col, N_COL * width))
```

```python
import functools

import jax
import jax.numpy as jnp
from jax import lax
from jax.experimental import pallas as pl
from jax.experimental.pallas import tpu as pltpu
from jax.sharding import PartitionSpec as P

LANES = 128
VM = pl.BlockSpec(memory_space=pltpu.VMEM)
SM = pl.BlockSpec(memory_space=pltpu.SMEM)


def nt(a, b, precision=None):
    return lax.dot_general(
        a, b, (((1,), (1,)), ((), ())), precision=precision, preferred_element_type=jnp.float32
    )


def split2(x):
    hi = x.astype(jnp.bfloat16)
    return hi, (x - hi.astype(jnp.float32)).astype(jnp.bfloat16)


def split3(x):
    hi, mid = split2(x)
    rest = x - hi.astype(jnp.float32) - mid.astype(jnp.float32)
    return hi, mid, rest.astype(jnp.bfloat16)


def pack_kernel(parity_ref, feat_ref, noise_ref, own_ref, oth_ref, first_ref, pad):
    width, depth = feat_ref.shape[1], feat_ref.shape[2]
    rest = LANES - depth
    pad[...] = jnp.zeros_like(pad)
    lane = lax.broadcasted_iota(jnp.int32, (width, LANES), 1)
    pad[:, 0:depth] = feat_ref[0].astype(jnp.float32)
    first_ref[0:width, :] = pad[...].astype(jnp.bfloat16)
    hi, mid, low = split3(noise_ref[0:1, :])
    row = lax.broadcasted_iota(jnp.int32, (16, LANES), 0)
    parts = jnp.where(row == 0, hi.astype(jnp.float32), 0.0)
    parts = jnp.where(row == 1, mid.astype(jnp.float32), parts)
    parts = jnp.where(row == 2, low.astype(jnp.float32), parts)
    first_ref[width : width + 16, :] = parts.astype(jnp.bfloat16)
    for out_ref, parity in ((own_ref, parity_ref[0]), (oth_ref, 1 - parity_ref[0])):
        pad[:, 0:depth] = feat_ref[6 + parity].astype(jnp.float32)
        last = pad[...]
        for k in range(3):
            pad[:, 0:depth] = feat_ref[2 * k + parity].astype(jnp.float32)
            moved = pltpu.roll(last, depth - rest * k, 1)
            out_ref[k * width : (k + 1) * width, :] = jnp.where(
                lane < depth, pad[...], moved
            ).astype(jnp.bfloat16)


def pack(parity, features, noise):
    width = features.shape[1]
    half = jax.ShapeDtypeStruct((3 * width, LANES), jnp.bfloat16)
    return pl.pallas_call(
        pack_kernel,
        out_shape=(half, half, jax.ShapeDtypeStruct((width + 16, LANES), jnp.bfloat16)),
        in_specs=[SM, VM, VM],
        out_specs=(VM, VM, VM),
        scratch_shapes=[pltpu.VMEM((width, LANES), jnp.float32)],
        name="pack",
    )(parity, features, noise)


def bcast(v):
    return jnp.broadcast_to(v, (8, LANES))


def inverse_factor(tiles, rows, lanes, m=8):
    size = 8 * len(tiles)
    tiles, out = list(tiles), [None] * len(tiles)
    for k in range(0, size, m):
        b, j = divmod(k, 8)
        r = [bcast(tiles[b][j + i : j + i + 1, :]) for i in range(m)]
        s = [[bcast(r[i][:, k + l : k + l + 1]) if l >= i else None for l in range(m)] for i in range(m)]
        r = [r[i] + jnp.where(lanes == k + i, 1.0, 0.0) for i in range(m)]
        inv, f = [], [[None] * m for _ in range(m)]
        for p in range(m):
            inv.append(1.0 / s[p][p])
            for i in range(p + 1, m):
                f[p][i] = s[p][i] * inv[p]
            for i in range(p + 1, m):
                for l in range(i, m):
                    s[i][l] = s[i][l] - f[p][i] * s[p][l]
            for i in range(p + 1, m):
                r[i] = r[i] - f[p][i] * r[p]
        for i in range(m):
            w = jnp.where(lanes < k + i, r[i], jnp.where(lanes == k + i, 1.0, 0.0)) * lax.rsqrt(s[i][i])
            out[b] = w if out[b] is None else jnp.where(rows == j + i, w, out[b])
        if k + m >= size:
            break
        y = [r[i] * inv[i] for i in range(m)]
        for i in range(m - 1, -1, -1):
            for l in range(i + 1, m):
                y[i] = y[i] - f[i][l] * y[l]
        for i in range(b, len(tiles)):
            if i == b and j + m >= 8:
                continue
            acc = None
            for q in range(m):
                c = bcast(tiles[i][:, k + q : k + q + 1])
                if i == b:
                    c = jnp.where(rows > j + m - 1, c, 0.0)
                acc = c * y[q] if acc is None else acc + c * y[q]
            tiles[i] = tiles[i] - acc
    return out


def first_kernel(weight_ref, *refs):
    pieces, (out_ref, work) = refs[:-2], refs[-2:]
    width = out_ref.shape[0]
    x = jnp.concatenate([piece[0:width, :] for piece in pieces], axis=1)
    w = jnp.concatenate([weight_ref[s : s + 1, :] for s in range(len(pieces))], axis=1)
    xf = x.astype(jnp.float32)
    xw = xf * w
    gram = sum(nt(x, part) for part in split3(xw))
    partial = jnp.zeros((width, LANES), jnp.float32)
    for s in range(len(pieces)):
        cut = slice(s * LANES, (s + 1) * LANES)
        partial = partial + xf[:, cut] * xw[:, cut]
    sq_col = jnp.sum(partial, axis=1, keepdims=True)
    sq_row = jnp.sum(partial.T, axis=0, keepdims=True)
    tail = pieces[0][width : width + 16, :].astype(jnp.float32)
    noise = tail[0:1, :] + tail[1:2, :] + tail[2:3, :]
    i = lax.broadcasted_iota(jnp.int32, (width, width), 0)
    j = lax.broadcasted_iota(jnp.int32, (width, width), 1)
    work[...] = jnp.exp(-0.5 * (sq_col + sq_row - 2.0 * gram)) + jnp.where(i == j, noise, 0.0)
    rows = lax.broadcasted_iota(jnp.int32, (8, LANES), 0)
    lanes = lax.broadcasted_iota(jnp.int32, (8, LANES), 1)
    tiles = [work[8 * t : 8 * t + 8, :] for t in range(width // 8)]
    for t, tile in enumerate(inverse_factor(tiles, rows, lanes)):
        out_ref[8 * t : 8 * t + 8, :] = tile


def first_tile(weight, pieces):
    width = pieces[0].shape[0] - 16
    return pl.pallas_call(
        first_kernel,
        out_shape=jax.ShapeDtypeStruct((width, width), jnp.float32),
        in_specs=[VM] * (1 + len(pieces)),
        out_specs=VM,
        scratch_shapes=[pltpu.VMEM((width, width), jnp.float32)],
        name="first_tile",
    )(weight, *pieces)


def unpack(blocks, depth):
    rest = LANES - depth
    lane = lax.broadcasted_iota(jnp.int32, blocks[0].shape, 1)
    tile = jnp.zeros(blocks[0].shape, jnp.float32)
    for k, block in enumerate(blocks):
        moved = pltpu.roll(block.astype(jnp.float32), LANES - depth + rest * k, 1)
        tile = jnp.where((lane >= rest * k) & (lane < rest * (k + 1)), moved, tile)
    return tile.astype(jnp.bfloat16)


def rest_kernel(depth, where_ref, weight_ref, noise_ref, inv_ref, *refs):
    n = 8
    firsts, refs = refs[:n], refs[n:]
    row_own, row_oth, cols = refs[:n], refs[n : 2 * n], refs[2 * n : 3 * n]
    panel_ref, trail_ref = refs[3 * n :]
    width = inv_ref.shape[0]
    parity, row_id, col_id, diag = where_ref[0], where_ref[1], where_ref[2], where_ref[3]
    highest = lax.Precision.HIGHEST

    def tile_of(refs_, t):
        parts = []
        for ref in refs_:
            if t < 3:
                parts.append(ref[t * width : (t + 1) * width, :])
            else:
                parts.append(unpack([ref[k * width : (k + 1) * width, :] for k in range(3)], depth))
        return jnp.concatenate(parts, axis=1)

    w = jnp.concatenate([weight_ref[s : s + 1, :] for s in range(n)], axis=1)

    def squares(xf, xw):
        partial = xf[:, 0:LANES] * xw[:, 0:LANES]
        for s in range(1, n):
            cut = slice(s * LANES, (s + 1) * LANES)
            partial = partial + xf[:, cut] * xw[:, cut]
        return partial

    def col_sum(partial):
        return jnp.sum(partial, axis=1, keepdims=True)

    def row_sum(partial):
        return jnp.sum(partial.T, axis=0, keepdims=True)

    eye = lax.broadcasted_iota(jnp.int32, (width, width), 0) == lax.broadcasted_iota(
        jnp.int32, (width, width), 1
    )
    tail = firsts[0][width : width + 16, :].astype(jnp.float32)
    noise0 = tail[0:1, :] + tail[1:2, :] + tail[2:3, :]
    diag0 = jnp.where(eye, noise0, 0.0)
    inv = inv_ref[...]

    a = jnp.concatenate([f[0:width, :] for f in firsts], axis=1)
    af = a.astype(jnp.float32)
    aw = af * w
    a_hi, a_lo = split2(aw)
    sq0 = row_sum(squares(af, aw))

    def panel_of(x, sq, first):
        gram = nt(x, a_hi) + nt(x, a_lo)
        kern = jnp.exp(-0.5 * (sq + sq0 - 2.0 * gram))
        kern = kern + jnp.where(first, diag0, 0.0)
        return nt(kern, inv, highest)

    c_hi, c_lo, c_sq, c_panel = [], [], [], []
    for t in range(4):
        c = tile_of(cols, t)
        cf = c.astype(jnp.float32)
        cw = cf * w
        partial = squares(cf, cw)
        hi, lo = split2(cw)
        c_hi.append(hi)
        c_lo.append(lo)
        c_sq.append(row_sum(partial))
        c_panel.append(panel_of(c, col_sum(partial), (col_id == 0) & (t == 0)))
    c_hi, c_lo = jnp.concatenate(c_hi, axis=0), jnp.concatenate(c_lo, axis=0)
    c_sq, c_panel = jnp.concatenate(c_sq, axis=1), jnp.concatenate(c_panel, axis=0)

    for t in range(4):
        for half, refs_ in enumerate((row_own, row_oth)):
            par = parity if half == 0 else 1 - parity
            tile = 2 * t + par
            x = tile_of(refs_, t)
            xf = x.astype(jnp.float32)
            sq = col_sum(squares(xf, xf * w))
            panel = panel_of(x, sq, (row_id == 0) & (tile == 0))
            panel_ref[tile] = panel
            gram = nt(x, c_hi) + nt(x, c_lo)
            kern = jnp.exp(-0.5 * (sq + c_sq - 2.0 * gram))
            trail = kern - nt(panel, c_panel, highest)
            for tc in range(4):
                block = trail[:, tc * width : (tc + 1) * width]
                if half == 0 and tc == t:
                    block = block + jnp.where(eye & (diag == 1), noise_ref[pl.ds(tile, 1), :], 0.0)
                trail_ref[pl.ds(tile * (4 * width) + tc, width, stride=4), :] = block


def rest(depth, where, weight, noise, inv, firsts, row_own, row_oth, cols):
    tiles, width = noise.shape
    return pl.pallas_call(
        functools.partial(rest_kernel, depth),
        out_shape=(
            jax.ShapeDtypeStruct((tiles, width, width), jnp.float32),
            jax.ShapeDtypeStruct((tiles * width * 4, width), jnp.float32),
        ),
        in_specs=[SM] + [VM] * (3 + 4 * 8),
        out_specs=(VM, VM),
        compiler_params=pltpu.CompilerParams(vmem_limit_bytes=48 * 1024 * 1024),
        name="rest",
    )(where, weight, noise, inv, *firsts, *row_own, *row_oth, *cols)


def body(features, lengthscale, noise):
    tiles, width, depth = features.shape
    row_id = lax.axis_index("row")
    col_id = lax.axis_index("col")
    n_rows, n_cols = lax.axis_size("row"), lax.axis_size("col")
    home = col_id % n_rows
    parity = col_id // n_rows

    def over_row(x, k):
        return lax.ppermute(x, "row", [(i, i ^ k) for i in range(n_rows)])

    def over_col(x, k):
        return lax.ppermute(x, "col", [(i, i ^ k) for i in range(n_cols)])

    own, oth, first = pack(parity.astype(jnp.int32).reshape(1), features, noise)
    firsts = [first] + [over_row(first, k) for k in (1, 2, 3)]
    first = lax.select_n(row_id, *firsts)
    mine = [first] + [over_col(first, 2 * k) for k in (1, 2, 3)]
    theirs = over_col(jnp.stack(mine), 1)
    firsts = mine + [theirs[k] for k in range(4)]
    order = col_id ^ jnp.array([0, 2, 4, 6, 1, 3, 5, 7], jnp.int32)
    inverse = 1.0 / lengthscale
    weight = jnp.pad((inverse * inverse).reshape(n_cols, depth), ((0, 0), (0, LANES - depth)))
    weight = jnp.take(weight, order, axis=0)
    inv = first_tile(weight, firsts)
    p = [own, over_col(own, 2), over_col(oth, 4), over_col(oth, 6)]
    q = [oth, over_col(oth, 2), over_col(own, 4), over_col(own, 6)]
    p_all, q_all = jnp.stack(p), jnp.stack(q)
    p_sib, q_sib = over_col(p_all, 1), over_col(q_all, 1)
    row_own = p + [p_sib[k] for k in range(4)]
    row_oth = q + [q_sib[k] for k in range(4)]
    near = [p_all] + [over_row(p_all, k) for k in (1, 2, 3)]
    keep = lax.select_n(row_id ^ home, *near)
    give = lax.select_n(row_id ^ home ^ 1, *near)
    give = over_col(give, 1)
    cols = [keep[k] for k in range(4)] + [give[k] for k in range(4)]
    where = jnp.stack([parity, row_id, col_id, (row_id == home).astype(jnp.int32)]).astype(jnp.int32)
    panel, trailing = rest(depth, where, weight, noise, inv, firsts, row_own, row_oth, cols)
    return panel, trailing.reshape(tiles, width, 4, width)


def from_root(block, axis, holder):
    block = jnp.where(lax.axis_index(axis) == holder, block, jnp.zeros_like(block))
    return lax.psum(block, axis)


def general_body(features, lengthscale, noise):
    rows_axis = lax.axis_size("row")
    cols_axis = lax.axis_size("col")
    row_id = lax.axis_index("row")
    col_id = lax.axis_index("col")
    tiles_row = features.shape[0]
    width = features.shape[1]
    stride = cols_axis // rows_axis
    tiles_col = tiles_row // stride
    row_feats = lax.all_gather(features, "col", axis=2, tiled=True)
    depth = row_feats.shape[2]
    grouped = row_feats.reshape(tiles_col, stride, width, depth)
    picked = lax.dynamic_index_in_dim(grouped, col_id // rows_axis, 1, keepdims=False)
    col_feats = from_root(picked, "row", col_id % rows_axis)
    inverse = 1.0 / lengthscale
    left = row_feats.reshape(tiles_row * width, depth).astype(jnp.float32) * inverse[None, :]
    right = col_feats.reshape(tiles_col * width, depth).astype(jnp.float32) * inverse[None, :]
    left_sq = jnp.sum(left * left, axis=1)
    right_sq = jnp.sum(right * right, axis=1)
    inner = jnp.arange(width, dtype=jnp.int32)
    row_index = (
        (jnp.arange(tiles_row, dtype=jnp.int32)[:, None] * rows_axis + row_id) * width + inner[None, :]
    ).reshape(-1)
    col_index = (
        (jnp.arange(tiles_col, dtype=jnp.int32)[:, None] * cols_axis + col_id) * width + inner[None, :]
    ).reshape(-1)
    gram = jnp.dot(left, right.T, precision=lax.Precision.HIGHEST)
    kern = jnp.exp(-0.5 * (left_sq[:, None] + right_sq[None, :] - 2.0 * gram))
    kern = kern + jnp.where(row_index[:, None] == col_index[None, :], noise.reshape(-1)[:, None], 0.0)
    diag_tile = from_root(kern[:width, :width], "row", 0)
    factor = jnp.linalg.cholesky(diag_tile)
    own_rows = jax.scipy.linalg.solve_triangular(factor, kern[:, :width].T, lower=True).T
    panel_rows = from_root(own_rows, "col", 0)
    panel_grouped = panel_rows.reshape(tiles_col, stride, width, width)
    panel_pick = lax.dynamic_index_in_dim(panel_grouped, col_id // rows_axis, 1, keepdims=False)
    panel_cols = from_root(panel_pick, "row", col_id % rows_axis).reshape(tiles_col * width, width)
    trailing = kern - jnp.dot(panel_rows, panel_cols.T, precision=lax.Precision.HIGHEST)
    return (
        panel_rows.reshape(tiles_row, width, width),
        trailing.reshape(tiles_row, width, tiles_col, width),
    )


def solution(mesh):
    placed = (P(None, "row", "col"), P(), P(None, "row"))
    small = mesh.shape["row"] == 4 and mesh.shape["col"] == 8
    return jax.shard_map(
        body if small else general_body,
        mesh=mesh,
        in_specs=placed,
        out_specs=(P(None, "row", None), P(None, "row", None, "col")),
        check_vma=False,
    )
```

```python
import functools

import jax
import jax.numpy as jnp
from jax import lax
from jax.experimental import pallas as pl
from jax.experimental.pallas import tpu as pltpu
from jax.sharding import PartitionSpec as P

LANES = 128
VMEM_ROWS = 28
VMEM_TRAIL = 32
ORDER = (0, 2, 4, 6, 1, 3, 5, 7)
VM = pl.BlockSpec(memory_space=pltpu.VMEM)
ANY = pl.BlockSpec(memory_space=pl.ANY)


def nt(a, b, precision=None):
    return lax.dot_general(
        a, b, (((1,), (1,)), ((), ())), precision=precision, preferred_element_type=jnp.float32
    )


def split2(x):
    hi = x.astype(jnp.bfloat16)
    return hi, (x - hi.astype(jnp.float32)).astype(jnp.bfloat16)


def split3(x):
    hi, mid = split2(x)
    rest = x - hi.astype(jnp.float32) - mid.astype(jnp.float32)
    return hi, mid, rest.astype(jnp.bfloat16)


def slice_weights(length_ref, depth):
    col_id = lax.axis_index("col")
    lane = lax.broadcasted_iota(jnp.int32, (8, LANES), 1)
    row = lax.broadcasted_iota(jnp.int32, (8, LANES), 0)
    held = jnp.ones((8, LANES), jnp.float32)
    for s in range(8):
        chunk, off = divmod(depth * s, LANES)
        here = jnp.broadcast_to(length_ref[chunk : chunk + 1, :], (8, LANES))
        if off:
            here = pltpu.roll(here, LANES - off, 1)
        if off + depth > LANES:
            more = jnp.broadcast_to(length_ref[chunk + 1 : chunk + 2, :], (8, LANES))
            here = jnp.where(lane < LANES - off, here, pltpu.roll(more, LANES - off, 1))
        for place, k in enumerate(ORDER):
            held = jnp.where((row == place) & (col_id == (s ^ k)), here, held)
    inverse = 1.0 / held
    columns = (inverse * inverse).T
    return [columns[0:depth, s : s + 1] for s in range(8)]


def bcast(v):
    return jnp.broadcast_to(v, (8, LANES))


def inverse_factor(tiles, rows, lanes, m=8):
    size = 8 * len(tiles)
    tiles, out = list(tiles), [None] * len(tiles)
    for k in range(0, size, m):
        b, j = divmod(k, 8)
        r = [bcast(tiles[b][j + i : j + i + 1, :]) for i in range(m)]
        s = [[bcast(r[i][:, k + l : k + l + 1]) if l >= i else None for l in range(m)] for i in range(m)]
        r = [r[i] + jnp.where(lanes == k + i, 1.0, 0.0) for i in range(m)]
        inv, f = [], [[None] * m for _ in range(m)]
        for p in range(m):
            inv.append(1.0 / s[p][p])
            for i in range(p + 1, m):
                f[p][i] = s[p][i] * inv[p]
            for i in range(p + 1, m):
                for l in range(i, m):
                    s[i][l] = s[i][l] - f[p][i] * s[p][l]
            for i in range(p + 1, m):
                r[i] = r[i] - f[p][i] * r[p]
        for i in range(m):
            w = jnp.where(lanes < k + i, r[i], jnp.where(lanes == k + i, 1.0, 0.0)) * lax.rsqrt(s[i][i])
            out[b] = w if out[b] is None else jnp.where(rows == j + i, w, out[b])
        if k + m >= size:
            break
        y = [r[i] * inv[i] for i in range(m)]
        for i in range(m - 1, -1, -1):
            for l in range(i + 1, m):
                y[i] = y[i] - f[i][l] * y[l]
        for i in range(b, len(tiles)):
            if i == b and j + m >= 8:
                continue
            acc = None
            for q in range(m):
                c = bcast(tiles[i][:, k + q : k + q + 1])
                if i == b:
                    c = jnp.where(rows > j + m - 1, c, 0.0)
                acc = c * y[q] if acc is None else acc + c * y[q]
            tiles[i] = tiles[i] - acc
    return out


def gather_kernel(feat_ref, near_ref, far1_ref, far2_ref, noise_ref, out_ref, land, sems):
    depth = feat_ref.shape[1]
    sources = (feat_ref.at[0], near_ref.at[0], far1_ref, far2_ref)
    copies = [pltpu.make_async_copy(src, land.at[k], sems.at[k]) for k, src in enumerate(sources)]
    for copy in copies:
        copy.start()
    row = lax.broadcasted_iota(jnp.int32, (16, LANES), 0)
    parts = jnp.zeros((16, LANES), jnp.float32)
    for k, part in enumerate(split3(noise_ref[0:1, :])):
        parts = jnp.where(row == k, part.astype(jnp.float32), parts)
    out_ref[4 * depth :, :] = parts.astype(jnp.bfloat16)
    for k, copy in enumerate(copies):
        copy.wait()
        out_ref[k * depth : (k + 1) * depth, :] = land[k]


def gather_first(feats, near, far, noise):
    _, depth, width = feats.shape
    return pl.pallas_call(
        gather_kernel,
        out_shape=jax.ShapeDtypeStruct((4 * depth + 16, width), jnp.bfloat16),
        in_specs=[ANY] * 4 + [VM],
        out_specs=VM,
        scratch_shapes=[pltpu.VMEM((4, depth, width), jnp.bfloat16), pltpu.SemaphoreType.DMA((4,))],
        name="gather_first",
    )(feats, near, *far, noise)


def first_kernel(length_ref, mine_ref, sib_ref, inv_ref, rows_ref, both_ref, sq_ref, diag_ref, work):
    width = inv_ref.shape[0]
    depth = (mine_ref.shape[0] - 16) // 4
    x = jnp.concatenate([ref[0 : 4 * depth, :] for ref in (mine_ref, sib_ref)], axis=0)
    w = jnp.concatenate(slice_weights(length_ref, depth), axis=0)
    xf = x.astype(jnp.float32)
    xw = xf * w
    parts = split3(xw)
    rows_ref[...] = xf.T.astype(jnp.bfloat16)
    both_ref[...] = jnp.concatenate(parts[:2], axis=1)
    gram = sum(
        lax.dot_general(rows_ref[...], part, (((1,), (0,)), ((), ())), preferred_element_type=jnp.float32)
        for part in parts
    )
    sq_row = jnp.sum(xf * xw, axis=0, keepdims=True)
    sq_ref[...] = jnp.broadcast_to(sq_row, sq_ref.shape)
    sq_col = jnp.broadcast_to(sq_row, (8, width)).T[:, 0:1]
    tail = mine_ref[4 * depth :, :].astype(jnp.float32)
    noise = tail[0:1, :] + tail[1:2, :] + tail[2:3, :]
    i = lax.broadcasted_iota(jnp.int32, (width, width), 0)
    j = lax.broadcasted_iota(jnp.int32, (width, width), 1)
    diag = jnp.where(i == j, noise, 0.0)
    diag_ref[...] = diag
    work[...] = jnp.exp(-0.5 * (sq_col + sq_row - 2.0 * gram)) + diag
    rows = lax.broadcasted_iota(jnp.int32, (8, LANES), 0)
    lanes = lax.broadcasted_iota(jnp.int32, (8, LANES), 1)
    tiles = [work[8 * t : 8 * t + 8, :] for t in range(width // 8)]
    for t, tile in enumerate(inverse_factor(tiles, rows, lanes)):
        inv_ref[8 * t : 8 * t + 8, :] = tile


def first_tile(lengths, mine, sib):
    width = mine.shape[1]
    whole = 2 * (mine.shape[0] - 16)
    return pl.pallas_call(
        first_kernel,
        out_shape=(
            jax.ShapeDtypeStruct((width, width), jnp.float32),
            jax.ShapeDtypeStruct((width, whole), jnp.bfloat16),
            jax.ShapeDtypeStruct((whole, 2 * width), jnp.bfloat16),
            jax.ShapeDtypeStruct((8, width), jnp.float32),
            jax.ShapeDtypeStruct((width, width), jnp.float32),
        ),
        in_specs=[VM] * 3,
        out_specs=(VM,) * 5,
        scratch_shapes=[pltpu.VMEM((width, width), jnp.float32)],
        name="first_tile",
    )(lengths, mine, sib)


def three(x):
    hi, lo = split2(x)
    return jnp.concatenate([hi, lo, hi], axis=1)


def twice(y):
    hi, lo = split2(y)
    return jnp.concatenate([hi, hi, lo], axis=1)


def twice_rows(y):
    hi, lo = split2(y)
    return jnp.concatenate([hi, hi, lo], axis=0)


def mm(a, b):
    return jnp.dot(a, b, preferred_element_type=jnp.float32)


def rows_kernel(length_ref, inv_ref, both_ref, sq0_ref, diag_ref, *refs):
    sources, (panel_ref, x_ref, sq_ref, land, sems) = refs[:4], refs[4:]
    depth, width = sources[0].shape[2:]
    copies = [
        [pltpu.make_async_copy(src.at[:, t], land.at[n, t], sems.at[n, t]) for n, src in enumerate(sources)]
        for t in range(4)
    ]
    for copy in sum(copies, []):
        copy.start()
    row_id, parity = lax.axis_index("row"), lax.axis_index("col") // lax.axis_size("row")
    w = jnp.concatenate(slice_weights(length_ref, depth), axis=0)
    inv = twice(inv_ref[...])
    for t in range(4):
        rows, sqs = [], []
        for copy in copies[t]:
            copy.wait()
        for n in (0, 2):
            xf = land[n : n + 2, t].reshape(8 * depth, width).astype(jnp.float32)
            rows.append(xf.T.astype(jnp.bfloat16))
            sq = jnp.sum(xf * xf * w, axis=0, keepdims=True)
            sqs.append(jnp.broadcast_to(sq, (LANES, width)).T)
        x, sq = jnp.concatenate(rows, axis=0), jnp.concatenate(sqs, axis=0)
        x_ref[2 * t * width : 2 * (t + 1) * width, :] = x
        sq_ref[2 * t * width : 2 * (t + 1) * width, :] = sq
        gram = mm(x, both_ref[...])
        gram = gram[:, 0:width] + gram[:, width:]
        kern = jnp.exp(gram - 0.5 * (sq + sq0_ref[0:1, :]))
        if t == 0:
            kern = jnp.concatenate(
                [
                    kern[h * width : (h + 1) * width]
                    + jnp.where((row_id == 0) & (parity == h), diag_ref[...], 0.0)
                    for h in range(2)
                ],
                axis=0,
            )
        panel = nt(three(kern), inv)
        panel_ref[2 * t + parity] = panel[0:width]
        panel_ref[2 * t + 1 - parity] = panel[width:]


def make_rows(lengths, first, *halves):
    inv, _, both, sq0, diag = first
    depth, width = halves[0].shape[2:]
    return pl.pallas_call(
        rows_kernel,
        out_shape=(
            jax.ShapeDtypeStruct((8, width, width), jnp.float32),
            jax.ShapeDtypeStruct((8 * width, 8 * depth), jnp.bfloat16),
            jax.ShapeDtypeStruct((8 * width, width), jnp.float32),
        ),
        in_specs=[VM] * 5 + [ANY] * 4,
        out_specs=(VM,) * 3,
        scratch_shapes=[
            pltpu.VMEM((4, 4, 4, depth, width), jnp.bfloat16),
            pltpu.SemaphoreType.DMA((4, 4)),
        ],
        compiler_params=pltpu.CompilerParams(vmem_limit_bytes=VMEM_ROWS * 1024 * 1024),
        name="rows",
    )(lengths, inv, both, sq0, diag, *halves)


def trail_kernel(length_ref, noise_ref, inv_ref, a_ref, sq0_ref, diag_ref, panel_ref, x_ref, sq_ref, *refs):
    sources, (trail_ref, land, sems) = refs[:2], refs[2:]
    depth, width = sources[0].shape[2:]
    copies = [
        [pltpu.make_async_copy(src.at[:, t], land.at[t, n], sems.at[t, n]) for n, src in enumerate(sources)]
        for t in range(4)
    ]
    for copy in sum(copies, []):
        copy.start()
    row_id, col_id, n_rows = lax.axis_index("row"), lax.axis_index("col"), lax.axis_size("row")
    parity, on_diag = col_id // n_rows, row_id == col_id % n_rows
    w = jnp.concatenate(slice_weights(length_ref, depth), axis=0)
    his, los, sqs = [], [], []
    for t in range(4):
        for copy in copies[t]:
            copy.wait()
        c = land[t].reshape(8 * depth, width).astype(jnp.float32)
        cw = c * w
        hi, lo = split2(cw)
        his.append(hi)
        los.append(lo)
        sqs.append(jnp.sum(c * cw, axis=0, keepdims=True))
    hi, lo = jnp.concatenate(his, axis=1), jnp.concatenate(los, axis=1)
    c_sq = 0.5 * jnp.concatenate(sqs, axis=1)

    eye = lax.broadcasted_iota(jnp.int32, (width, width), 0) == lax.broadcasted_iota(
        jnp.int32, (width, width), 1
    )
    sq0 = sq0_ref[...].T[:, 0:1]
    kern = jnp.exp(mm(a_ref[...], hi) + mm(a_ref[...], lo) - (0.5 * sq0 + c_sq))
    kern = jnp.concatenate(
        [kern[:, 0:width] + jnp.where(col_id == 0, diag_ref[...], 0.0), kern[:, width:]], axis=1
    )
    c_panel = twice_rows(mm(three(inv_ref[...]), twice_rows(kern)))

    for t in range(4):
        x = x_ref[2 * t * width : 2 * (t + 1) * width, :]
        sq = sq_ref[2 * t * width : 2 * (t + 1) * width, 0:1]
        panel = jnp.concatenate([panel_ref[2 * t + parity], panel_ref[2 * t + 1 - parity]], axis=0)
        kern = jnp.exp(mm(x, hi) + mm(x, lo) - (0.5 * sq + c_sq))
        trail = kern - mm(three(panel), c_panel)
        for half in range(2):
            tile = 2 * t + (parity if half == 0 else 1 - parity)
            for tc in range(4):
                block = trail[half * width : (half + 1) * width, tc * width : (tc + 1) * width]
                if half == 0 and tc == t:
                    block = block + jnp.where(eye & on_diag, noise_ref[pl.ds(tile, 1), :], 0.0)
                trail_ref[pl.ds(tile * (4 * width) + tc, width, stride=4), :] = block


def make_trail(lengths, noise, first, rows, *cols):
    inv, a, _, sq0, diag = first
    tiles, width = noise.shape
    depth = cols[0].shape[2]
    return pl.pallas_call(
        trail_kernel,
        out_shape=jax.ShapeDtypeStruct((tiles * width * 4, width), jnp.float32),
        in_specs=[VM] * 9 + [ANY] * 2,
        out_specs=VM,
        scratch_shapes=[
            pltpu.VMEM((4, 2, 4, depth, width), jnp.bfloat16),
            pltpu.SemaphoreType.DMA((4, 2)),
        ],
        compiler_params=pltpu.CompilerParams(vmem_limit_bytes=VMEM_TRAIL * 1024 * 1024),
        name="trail",
    )(lengths, noise, inv, a, sq0, diag, *rows, *cols)


def body(features, lengthscale, noise):
    tiles, width, depth = features.shape
    row_id = lax.axis_index("row")
    col_id = lax.axis_index("col")
    n_rows, n_cols = lax.axis_size("row"), lax.axis_size("col")
    home = col_id % n_rows
    parity = col_id // n_rows

    def over_row(x, k):
        return lax.ppermute(x, "row", [(i, i ^ k) for i in range(n_rows)])

    def over_col(x, k):
        return lax.ppermute(x, "col", [(i, i ^ k) for i in range(n_cols)])

    feats = jnp.transpose(features, (0, 2, 1))
    lengths = lengthscale.reshape(-1, LANES)
    halves = feats.reshape(4, 2, depth, width)
    own = lax.dynamic_index_in_dim(halves, parity, 1, keepdims=False)
    oth = lax.dynamic_index_in_dim(halves, 1 - parity, 1, keepdims=False)
    near = over_col(feats, 2)
    far = [over_col(feats[0], 2 * k) for k in (2, 3)]
    near_own = lax.dynamic_index_in_dim(near.reshape(halves.shape), parity, 1, keepdims=False)
    near_oth = lax.dynamic_index_in_dim(near.reshape(halves.shape), 1 - parity, 1, keepdims=False)
    oth_late, far[0], far[1] = lax.optimization_barrier((oth, *far))
    p = [own, near_own, over_col(oth_late, 4), over_col(oth_late, 6)]
    stack = gather_first(feats, near, far, noise)
    stack = lax.select_n(row_id, stack, *[over_row(stack, k) for k in (1, 2, 3)])
    sib = over_col(stack, 1)
    first = first_tile(lengths, stack, sib)
    p_all, stack = lax.optimization_barrier((jnp.stack(p), stack))
    planes = [p_all] + [over_row(p_all, k) for k in (1, 2, 3)]
    own_late, _ = lax.optimization_barrier((own, sib))
    q_all = jnp.stack([oth, near_oth, over_col(own_late, 4), over_col(own_late, 6)])
    p_late, q_late, _ = lax.optimization_barrier((p_all, q_all, first[0]))
    rows = make_rows(lengths, first, p_late, over_col(p_late, 1), q_late, over_col(q_late, 1))
    keep = lax.select_n(row_id ^ home, *planes)
    give = over_col(lax.select_n(row_id ^ home ^ 1, *planes), 1)
    trailing = make_trail(lengths, noise, first, rows, keep, give)
    return rows[0], trailing.reshape(tiles, width, 4, width)


def from_root(block, axis, holder):
    block = jnp.where(lax.axis_index(axis) == holder, block, jnp.zeros_like(block))
    return lax.psum(block, axis)


def general_body(features, lengthscale, noise):
    rows_axis = lax.axis_size("row")
    cols_axis = lax.axis_size("col")
    row_id = lax.axis_index("row")
    col_id = lax.axis_index("col")
    tiles_row = features.shape[0]
    width = features.shape[1]
    stride = cols_axis // rows_axis
    tiles_col = tiles_row // stride
    row_feats = lax.all_gather(features, "col", axis=2, tiled=True)
    depth = row_feats.shape[2]
    grouped = row_feats.reshape(tiles_col, stride, width, depth)
    picked = lax.dynamic_index_in_dim(grouped, col_id // rows_axis, 1, keepdims=False)
    col_feats = from_root(picked, "row", col_id % rows_axis)
    inverse = 1.0 / lengthscale
    left = row_feats.reshape(tiles_row * width, depth).astype(jnp.float32) * inverse[None, :]
    right = col_feats.reshape(tiles_col * width, depth).astype(jnp.float32) * inverse[None, :]
    left_sq = jnp.sum(left * left, axis=1)
    right_sq = jnp.sum(right * right, axis=1)
    inner = jnp.arange(width, dtype=jnp.int32)
    row_index = (
        (jnp.arange(tiles_row, dtype=jnp.int32)[:, None] * rows_axis + row_id) * width + inner[None, :]
    ).reshape(-1)
    col_index = (
        (jnp.arange(tiles_col, dtype=jnp.int32)[:, None] * cols_axis + col_id) * width + inner[None, :]
    ).reshape(-1)
    gram = jnp.dot(left, right.T, precision=lax.Precision.HIGHEST)
    kern = jnp.exp(-0.5 * (left_sq[:, None] + right_sq[None, :] - 2.0 * gram))
    kern = kern + jnp.where(row_index[:, None] == col_index[None, :], noise.reshape(-1)[:, None], 0.0)
    diag_tile = from_root(kern[:width, :width], "row", 0)
    factor = jnp.linalg.cholesky(diag_tile)
    own_rows = jax.scipy.linalg.solve_triangular(factor, kern[:, :width].T, lower=True).T
    panel_rows = from_root(own_rows, "col", 0)
    panel_grouped = panel_rows.reshape(tiles_col, stride, width, width)
    panel_pick = lax.dynamic_index_in_dim(panel_grouped, col_id // rows_axis, 1, keepdims=False)
    panel_cols = from_root(panel_pick, "row", col_id % rows_axis).reshape(tiles_col * width, width)
    trailing = kern - jnp.dot(panel_rows, panel_cols.T, precision=lax.Precision.HIGHEST)
    return (
        panel_rows.reshape(tiles_row, width, width),
        trailing.reshape(tiles_row, width, tiles_col, width),
    )


def solution(mesh):
    placed = (P(None, "row", "col"), P(), P(None, "row"))
    small = mesh.shape["row"] == 4 and mesh.shape["col"] == 8
    return jax.shard_map(
        body if small else general_body,
        mesh=mesh,
        in_specs=placed,
        out_specs=(P(None, "row", None), P(None, "row", None, "col")),
        check_vma=False,
    )
```

```python
import functools

import jax
import jax.numpy as jnp
from jax import lax
from jax.experimental import pallas as pl
from jax.experimental.pallas import tpu as pltpu
from jax.sharding import PartitionSpec as P

LANES = 128
VMEM_REST = 32
ORDER = (0, 2, 4, 6, 1, 3, 5, 7)
VM = pl.BlockSpec(memory_space=pltpu.VMEM)


def nt(a, b, precision=None):
    return lax.dot_general(
        a, b, (((1,), (1,)), ((), ())), precision=precision, preferred_element_type=jnp.float32
    )


def split2(x):
    hi = x.astype(jnp.bfloat16)
    return hi, (x - hi.astype(jnp.float32)).astype(jnp.bfloat16)


def split3(x):
    hi, mid = split2(x)
    rest = x - hi.astype(jnp.float32) - mid.astype(jnp.float32)
    return hi, mid, rest.astype(jnp.bfloat16)


def pack_kernel(feat_ref, both_ref, own_ref, oth_ref):
    tiles, depth, width = feat_ref.shape
    left = LANES - depth
    parity = lax.axis_index("col") // lax.axis_size("row")
    for half, out_ref in ((0, own_ref), (1, oth_ref)):
        tile = [feat_ref[2 * k + (parity if half == 0 else 1 - parity)] for k in range(4)]
        for k in range(3):
            block = jnp.concatenate([tile[k], tile[3][left * k : left * (k + 1)]], axis=0).T
            out_ref[k * width : (k + 1) * width, :] = block
            both_ref[(3 * half + k) * width : (3 * half + k + 1) * width, :] = block


def pack(feats):
    width = feats.shape[2]
    half = jax.ShapeDtypeStruct((3 * width, width), jnp.bfloat16)
    return pl.pallas_call(
        pack_kernel,
        out_shape=(jax.ShapeDtypeStruct((6 * width, width), jnp.bfloat16), half, half),
        in_specs=[VM],
        out_specs=(VM,) * 3,
        name="pack",
    )(feats)


def slice_weights(length_ref, depth):
    col_id = lax.axis_index("col")
    lane = lax.broadcasted_iota(jnp.int32, (8, LANES), 1)
    row = lax.broadcasted_iota(jnp.int32, (8, LANES), 0)
    held = jnp.ones((8, LANES), jnp.float32)
    for s in range(8):
        chunk, off = divmod(depth * s, LANES)
        here = jnp.broadcast_to(length_ref[chunk : chunk + 1, :], (8, LANES))
        if off:
            here = pltpu.roll(here, LANES - off, 1)
        if off + depth > LANES:
            more = jnp.broadcast_to(length_ref[chunk + 1 : chunk + 2, :], (8, LANES))
            here = jnp.where(lane < LANES - off, here, pltpu.roll(more, LANES - off, 1))
        for place, k in enumerate(ORDER):
            held = jnp.where((row == place) & (col_id == (s ^ k)), here, held)
    inverse = 1.0 / held
    columns = (inverse * inverse).T
    return [columns[0:depth, s : s + 1] for s in range(8)]


def bcast(v):
    return jnp.broadcast_to(v, (8, LANES))


def inverse_factor(tiles, rows, lanes, m=8, g=4):
    size = 8 * len(tiles)
    tiles, out = list(tiles), [None] * len(tiles)

    def total(terms):
        while len(terms) > 1:
            terms = [sum(terms[z : z + 2]) for z in range(0, len(terms), 2)]
        return terms[0]

    for k in range(0, size, m):
        b, j = divmod(k, 8)
        r = [bcast(tiles[b][j + i : j + i + 1, :]) for i in range(m)]
        s = [[bcast(r[i][:, k + l : k + l + 1]) if l >= i else None for l in range(m)] for i in range(m)]
        r = [r[i] + jnp.where(lanes == k + i, 1.0, 0.0) for i in range(m)]
        inv = [None] * m
        for q in range(0, m, g):
            scale, roots = None, []
            for p in range(q, q + g):
                product = s[p][p] if scale is None else scale * s[p][p]
                root = lax.rsqrt(product)
                inv[p] = root if scale is None else root * scale
                roots.append(root)
                for i in range(p + 1, q + g):
                    for l in range(m - 1, i - 1, -1):
                        s[i][l] = s[p][p] * s[i][l] - s[p][i] * s[p][l]
                    r[i] = s[p][p] * r[i] - s[p][i] * r[p]
                scale = product
            for p in range(q, q + g):
                r[p] = r[p] * roots[p - q]
                for l in range(p + 1, m):
                    s[p][l] = s[p][l] * roots[p - q]
            for i in range(q + g, m):
                for l in range(i, m):
                    s[i][l] = s[i][l] - total([s[p][i] * s[p][l] for p in range(q, q + g)])
                r[i] = r[i] - total([s[p][i] * r[p] for p in range(q, q + g)])
        for i in range(m):
            w = jnp.where(lanes < k + i, r[i], jnp.where(lanes == k + i, inv[i], 0.0))
            out[b] = w if out[b] is None else jnp.where(rows == j + i, w, out[b])
        if k + m >= size:
            break
        y = [r[i] * inv[i] for i in range(m)]
        for i in range(m):
            for l in range(i + 1, m):
                s[i][l] = s[i][l] * inv[i]
        for l in range(m - 1, 0, -1):
            for i in range(l - 1, -1, -1):
                y[i] = y[i] - s[i][l] * y[l]
        for i in range(b, len(tiles)):
            if i == b and j + m >= 8:
                continue
            terms = []
            for q in range(m):
                c = bcast(tiles[i][:, k + q : k + q + 1])
                if i == b:
                    c = jnp.where(rows > j + m - 1, c, 0.0)
                terms.append(c * y[q])
            tiles[i] = tiles[i] - total(terms)
    return out


def dense_rows(x, depth):
    left = LANES - depth
    blocks = []
    for g in range(0, 8, 4):
        for b in range(3):
            blocks.append(x[(g + b) * depth : (g + b + 1) * depth])
            last = (g + 3) * depth + left * b
            blocks.append(x[last : last + left])
    return jnp.concatenate(blocks, axis=0)


def first_kernel(length_ref, mine_ref, sib_ref, inv_ref, both_ref, sq_ref, diag_ref, work):
    width = inv_ref.shape[0]
    depth = (mine_ref.shape[0] - 16) // 4
    x = jnp.concatenate([ref[0 : 4 * depth, :] for ref in (mine_ref, sib_ref)], axis=0)
    w = jnp.concatenate(slice_weights(length_ref, depth), axis=0)
    xf = x.astype(jnp.float32)
    xw = xf * w
    parts = split3(xw)
    both_ref[...] = dense_rows(jnp.concatenate(parts[:2], axis=1), depth)
    turned = x.T
    gram = sum(jnp.dot(turned, part, preferred_element_type=jnp.float32) for part in parts)
    sq_row = jnp.sum(xf * xw, axis=0, keepdims=True)
    sq_ref[...] = jnp.broadcast_to(sq_row, sq_ref.shape)
    sq_col = jnp.broadcast_to(sq_row, (8, width)).T[:, 0:1]
    tail = mine_ref[4 * depth :, :].astype(jnp.float32)
    noise = tail[0:1, :] + tail[1:2, :] + tail[2:3, :]
    i = lax.broadcasted_iota(jnp.int32, (width, width), 0)
    j = lax.broadcasted_iota(jnp.int32, (width, width), 1)
    diag = jnp.where(i == j, noise, 0.0)
    diag_ref[...] = diag
    work[...] = jnp.exp(-0.5 * (sq_col + sq_row - 2.0 * gram)) + diag
    rows = lax.broadcasted_iota(jnp.int32, (8, LANES), 0)
    lanes = lax.broadcasted_iota(jnp.int32, (8, LANES), 1)
    tiles = [work[8 * t : 8 * t + 8, :] for t in range(width // 8)]
    for t, tile in enumerate(inverse_factor(tiles, rows, lanes)):
        inv_ref[8 * t : 8 * t + 8, :] = tile


def first_tile(lengths, mine, sib):
    width = mine.shape[1]
    whole = 2 * (mine.shape[0] - 16)
    return pl.pallas_call(
        first_kernel,
        out_shape=(
            jax.ShapeDtypeStruct((width, width), jnp.float32),
            jax.ShapeDtypeStruct((whole, 2 * width), jnp.bfloat16),
            jax.ShapeDtypeStruct((8, width), jnp.float32),
            jax.ShapeDtypeStruct((width, width), jnp.float32),
        ),
        in_specs=[VM] * 3,
        out_specs=(VM,) * 4,
        scratch_shapes=[pltpu.VMEM((width, width), jnp.float32)],
        name="first_tile",
    )(lengths, mine, sib)


def dense(refs, t, width, depth):
    left = LANES - depth
    lane = lax.broadcasted_iota(jnp.int32, (width, LANES), 1)
    blocks = []
    for g in range(0, 8, 4):
        if t < 3:
            parts = [ref[t * width : (t + 1) * width, :] for ref in refs[g : g + 4]]
            for b in range(3):
                moved = pltpu.roll(parts[3], depth - left * b, 1)
                blocks.append(jnp.where(lane < depth, parts[b], moved))
        else:
            for b in range(3):
                block = refs[g + 3][b * width : (b + 1) * width, :]
                for k in range(3):
                    moved = pltpu.roll(
                        refs[g + b][k * width : (k + 1) * width, :], LANES - depth + left * k, 1
                    )
                    block = jnp.where((lane >= left * k) & (lane < left * (k + 1)), moved, block)
                blocks.append(block)
    return jnp.concatenate(blocks, axis=1)


def dense_weights(length_ref, depth):
    parts = dense_rows(jnp.concatenate(slice_weights(length_ref, depth), axis=0), depth)
    return jnp.broadcast_to(parts, (8 * depth, LANES)).T[0:1, :]


def three(x):
    hi, lo = split2(x)
    return jnp.concatenate([hi, lo, hi], axis=1)


def twice(y):
    hi, lo = split2(y)
    return jnp.concatenate([hi, hi, lo], axis=1)


def rest_kernel(depth, length_ref, noise_ref, inv_ref, both_ref, sq0_ref, diag_ref, *refs):
    row_refs, col_refs, (panel_ref, trail_ref) = refs[:9], refs[9:13], refs[13:]
    width = inv_ref.shape[0]
    h = 3 * width
    w0, w1, p, q2, q3, s0, s1, sp, sq = row_refs
    third = lambda ref, k: ref.at[pl.ds(k * h, h)]
    row_own = [third(w0, 0), third(w1, 0), third(p, 1), third(p, 2)]
    row_own += [third(s0, 0), third(s1, 0), third(sp, 1), third(sp, 2)]
    row_oth = [third(w0, 1), third(w1, 1), q2, q3, third(s0, 1), third(s1, 1), third(sq, 0), third(sq, 1)]
    cols = []
    for near, far in (col_refs[0:2], col_refs[2:4]):
        cols += [near, third(far, 0), third(far, 1), third(far, 2)]
    row_id, col_id, n_rows = lax.axis_index("row"), lax.axis_index("col"), lax.axis_size("row")
    parity, on_diag = col_id // n_rows, row_id == col_id % n_rows

    w = dense_weights(length_ref, depth)
    blocks = w.shape[1] // LANES

    def squares(xf, xw):
        partial = xf[:, 0:LANES] * xw[:, 0:LANES]
        for s in range(1, blocks):
            cut = slice(s * LANES, (s + 1) * LANES)
            partial = partial + xf[:, cut] * xw[:, cut]
        return partial

    eye = lax.broadcasted_iota(jnp.int32, (width, width), 0) == lax.broadcasted_iota(
        jnp.int32, (width, width), 1
    )
    inv = twice(inv_ref[...])
    sq0 = sq0_ref[0:1, :]

    def panel_of(x, sq, heads):
        gram = jnp.dot(x, both_ref[...], preferred_element_type=jnp.float32)
        gram = gram[:, 0:width] + gram[:, width:]
        kern = jnp.exp(gram - 0.5 * (sq + sq0))
        if heads:
            tops = [
                kern[h * width : (h + 1) * width] + jnp.where(c, diag_ref[...], 0.0)
                for h, c in enumerate(heads)
            ]
            if len(heads) * width < kern.shape[0]:
                tops.append(kern[len(heads) * width :])
            kern = jnp.concatenate(tops, axis=0)
        return nt(three(kern), inv)

    c_hi, c_lo, c_sq, c_panel = [], [], [], []
    for t in range(4):
        c = dense(cols, t, width, depth)
        cf = c.astype(jnp.float32)
        cw = cf * w
        partial = squares(cf, cw)
        hi, lo = split2(cw)
        c_hi.append(hi)
        c_lo.append(lo)
        c_sq.append(jnp.sum(partial.T, axis=0, keepdims=True))
        sq = jnp.sum(partial, axis=1, keepdims=True)
        c_panel.append(panel_of(c, sq, [col_id == 0] if t == 0 else []))
    c_hi, c_lo = jnp.concatenate(c_hi, axis=0), jnp.concatenate(c_lo, axis=0)
    c_sq = jnp.concatenate(c_sq, axis=1)
    c_panel = twice(jnp.concatenate(c_panel, axis=0))

    for t in range(4):
        x = jnp.concatenate([dense(row_own, t, width, depth), dense(row_oth, t, width, depth)], axis=0)
        xf = x.astype(jnp.float32)
        sq = jnp.sum(squares(xf, xf * w), axis=1, keepdims=True)
        heads = [(row_id == 0) & (parity == h) for h in range(2)] if t == 0 else []
        panel = panel_of(x, sq, heads)
        gram = nt(x, c_hi) + nt(x, c_lo)
        kern = jnp.exp(gram - 0.5 * (sq + c_sq))
        trail = kern - nt(three(panel), c_panel)
        for half in range(2):
            tile = 2 * t + (parity if half == 0 else 1 - parity)
            low = half * width
            panel_ref[tile] = panel[low : low + width]
            for tc in range(4):
                block = trail[low : low + width, tc * width : (tc + 1) * width]
                if half == 0 and tc == t:
                    block = block + jnp.where(eye & on_diag, noise_ref[pl.ds(tile, 1), :], 0.0)
                trail_ref[pl.ds(tile * (4 * width) + tc, width, stride=4), :] = block


def rest(depth, lengths, noise, first, *slices):
    tiles, width = noise.shape
    return pl.pallas_call(
        functools.partial(rest_kernel, depth),
        out_shape=(
            jax.ShapeDtypeStruct((tiles, width, width), jnp.float32),
            jax.ShapeDtypeStruct((tiles * width * 4, width), jnp.float32),
        ),
        in_specs=[VM] * 19,
        out_specs=(VM, VM),
        compiler_params=pltpu.CompilerParams(vmem_limit_bytes=VMEM_REST * 1024 * 1024),
        name="rest",
    )(lengths, noise, *first, *slices)


def noise_parts(noise):
    rest, parts = noise[0:1], []
    for _ in range(3):
        part = lax.reduce_precision(rest, 8, 7)
        parts.append(part.astype(jnp.bfloat16))
        rest = rest - part
    return jnp.concatenate(parts + [jnp.zeros((13, noise.shape[1]), jnp.bfloat16)], axis=0)


def body(features, lengthscale, noise):
    tiles, width, depth = features.shape
    row_id = lax.axis_index("row")
    col_id = lax.axis_index("col")
    n_rows, n_cols = lax.axis_size("row"), lax.axis_size("col")
    home = col_id % n_rows
    parity = col_id // n_rows

    def over_row(x, k):
        return lax.ppermute(x, "row", [(i, i ^ k) for i in range(n_rows)])

    def over_col(x, k):
        return lax.ppermute(x, "col", [(i, i ^ k) for i in range(n_cols)])

    feats = jnp.transpose(features, (0, 2, 1))
    lengths = lengthscale.reshape(-1, LANES)

    def after(x, *others):
        return lax.optimization_barrier((x, *others))[0]

    head = feats[0]
    far = [over_col(head, 2 * k) for k in (1, 2, 3)]
    both, own, oth = pack(after(feats, head))
    both, oth, *far = lax.optimization_barrier((both, oth, *far))
    near, p2, p3 = over_col(both, 2), over_col(oth, 4), over_col(oth, 6)
    size, low = own.shape[0], 4 * depth + 16
    early = jnp.concatenate([head] + far + [noise_parts(noise), own], axis=0)
    early = [early] + [over_row(early, k) for k in (1, 2, 3)]
    *early, p2, p3 = lax.optimization_barrier((*early, p2, p3))
    stack = lax.select_n(row_id, *[v[:low] for v in early])
    sib = over_col(stack, 1)
    p = jnp.concatenate([near[:size], p2, p3], axis=0)
    planes = [p] + [over_row(p, k) for k in (1, 2, 3)]
    own_late = after(own, sib)
    q2, q3 = over_col(own_late, 4), over_col(own_late, 6)
    first = first_tile(lengths, stack, sib)
    q2, q3, *planes, sib_both, sib_near, sib_p, _ = lax.optimization_barrier(
        (q2, q3, *planes, both, near, p, first[0])
    )
    sib_both, sib_near, sib_p = (over_col(v, 1) for v in (sib_both, sib_near, sib_p))
    sib_q = over_col(jnp.concatenate([q2, q3], axis=0), 1)
    early = [v[low:] for v in early]
    take = lambda k: [lax.select_n(k, *v) for v in (early, planes)]
    keep = take(row_id ^ home)
    give = [over_col(v, 1) for v in take(row_id ^ home ^ 1)]
    panel, trailing = rest(
        depth, lengths, noise, first, both, near, p, q2, q3, sib_both, sib_near, sib_p, sib_q, *keep, *give
    )
    return panel, trailing.reshape(tiles, width, 4, width)


def from_root(block, axis, holder):
    block = jnp.where(lax.axis_index(axis) == holder, block, jnp.zeros_like(block))
    return lax.psum(block, axis)


def general_body(features, lengthscale, noise):
    rows_axis = lax.axis_size("row")
    cols_axis = lax.axis_size("col")
    row_id = lax.axis_index("row")
    col_id = lax.axis_index("col")
    tiles_row = features.shape[0]
    width = features.shape[1]
    stride = cols_axis // rows_axis
    tiles_col = tiles_row // stride
    row_feats = lax.all_gather(features, "col", axis=2, tiled=True)
    depth = row_feats.shape[2]
    grouped = row_feats.reshape(tiles_col, stride, width, depth)
    picked = lax.dynamic_index_in_dim(grouped, col_id // rows_axis, 1, keepdims=False)
    col_feats = from_root(picked, "row", col_id % rows_axis)
    inverse = 1.0 / lengthscale
    left = row_feats.reshape(tiles_row * width, depth).astype(jnp.float32) * inverse[None, :]
    right = col_feats.reshape(tiles_col * width, depth).astype(jnp.float32) * inverse[None, :]
    left_sq = jnp.sum(left * left, axis=1)
    right_sq = jnp.sum(right * right, axis=1)
    inner = jnp.arange(width, dtype=jnp.int32)
    row_index = (
        (jnp.arange(tiles_row, dtype=jnp.int32)[:, None] * rows_axis + row_id) * width + inner[None, :]
    ).reshape(-1)
    col_index = (
        (jnp.arange(tiles_col, dtype=jnp.int32)[:, None] * cols_axis + col_id) * width + inner[None, :]
    ).reshape(-1)
    gram = jnp.dot(left, right.T, precision=lax.Precision.HIGHEST)
    kern = jnp.exp(-0.5 * (left_sq[:, None] + right_sq[None, :] - 2.0 * gram))
    kern = kern + jnp.where(row_index[:, None] == col_index[None, :], noise.reshape(-1)[:, None], 0.0)
    diag_tile = from_root(kern[:width, :width], "row", 0)
    factor = jnp.linalg.cholesky(diag_tile)
    own_rows = jax.scipy.linalg.solve_triangular(factor, kern[:, :width].T, lower=True).T
    panel_rows = from_root(own_rows, "col", 0)
    panel_grouped = panel_rows.reshape(tiles_col, stride, width, width)
    panel_pick = lax.dynamic_index_in_dim(panel_grouped, col_id // rows_axis, 1, keepdims=False)
    panel_cols = from_root(panel_pick, "row", col_id % rows_axis).reshape(tiles_col * width, width)
    trailing = kern - jnp.dot(panel_rows, panel_cols.T, precision=lax.Precision.HIGHEST)
    return (
        panel_rows.reshape(tiles_row, width, width),
        trailing.reshape(tiles_row, width, tiles_col, width),
    )


def solution(mesh):
    placed = (P(None, "row", "col"), P(), P(None, "row"))
    small = mesh.shape["row"] == 4 and mesh.shape["col"] == 8
    return jax.shard_map(
        body if small else general_body,
        mesh=mesh,
        in_specs=placed,
        out_specs=(P(None, "row", None), P(None, "row", None, "col")),
        check_vma=False,
    )
```

```python
import functools

import jax
import jax.numpy as jnp
from jax import lax
from jax.experimental import pallas as pl
from jax.experimental.pallas import tpu as pltpu
from jax.sharding import PartitionSpec as P

LANES = 128
VMEM_REST = 32
ORDER = (0, 2, 4, 6, 1, 3, 5, 7)
VM = pl.BlockSpec(memory_space=pltpu.VMEM)
ANY = pl.BlockSpec(memory_space=pl.ANY)


def nt(a, b, precision=None):
    return lax.dot_general(
        a, b, (((1,), (1,)), ((), ())), precision=precision, preferred_element_type=jnp.float32
    )


def split2(x):
    hi = x.astype(jnp.bfloat16)
    return hi, (x - hi.astype(jnp.float32)).astype(jnp.bfloat16)


def split3(x):
    hi, mid = split2(x)
    rest = x - hi.astype(jnp.float32) - mid.astype(jnp.float32)
    return hi, mid, rest.astype(jnp.bfloat16)


def pack_kernel(feat_ref, noise_ref, own_ref, oth_ref, own_long_ref, oth_long_ref):
    tiles, depth, width = feat_ref.shape
    left = LANES - depth
    parity = lax.axis_index("col") // lax.axis_size("row")
    for half, outs in ((0, (own_ref, own_long_ref)), (1, (oth_ref, oth_long_ref))):
        tile = [feat_ref[2 * k + (parity if half == 0 else 1 - parity)] for k in range(4)]
        for k in range(3):
            block = jnp.concatenate([tile[k], tile[3][left * k : left * (k + 1)]], axis=0).T
            for out_ref in outs:
                out_ref[k * width : (k + 1) * width, :] = block
    row = lax.broadcasted_iota(jnp.int32, (16, width), 0)
    parts = jnp.zeros((16, width), jnp.float32)
    for k, part in enumerate(split3(noise_ref[0:1, :])):
        parts = jnp.where(row == k, part.astype(jnp.float32), parts)
    for out_ref in (own_long_ref, oth_long_ref):
        out_ref[3 * width : 3 * width + depth, :] = feat_ref[0]
        out_ref[3 * width + depth :, :] = parts.astype(jnp.bfloat16)


def pack(feats, noise):
    _, depth, width = feats.shape
    rows = lambda n: jax.ShapeDtypeStruct((n, width), jnp.bfloat16)
    return pl.pallas_call(
        pack_kernel,
        out_shape=(
            rows(3 * width),
            rows(3 * width),
            rows(3 * width + depth + 16),
            rows(3 * width + depth + 16),
        ),
        in_specs=[VM, VM],
        out_specs=(VM,) * 4,
        name="pack",
    )(feats, noise)


def slice_weights(length_ref, depth):
    col_id = lax.axis_index("col")
    lane = lax.broadcasted_iota(jnp.int32, (8, LANES), 1)
    row = lax.broadcasted_iota(jnp.int32, (8, LANES), 0)
    held = jnp.ones((8, LANES), jnp.float32)
    for s in range(8):
        chunk, off = divmod(depth * s, LANES)
        here = jnp.broadcast_to(length_ref[chunk : chunk + 1, :], (8, LANES))
        if off:
            here = pltpu.roll(here, LANES - off, 1)
        if off + depth > LANES:
            more = jnp.broadcast_to(length_ref[chunk + 1 : chunk + 2, :], (8, LANES))
            here = jnp.where(lane < LANES - off, here, pltpu.roll(more, LANES - off, 1))
        for place, k in enumerate(ORDER):
            held = jnp.where((row == place) & (col_id == (s ^ k)), here, held)
    inverse = 1.0 / held
    columns = (inverse * inverse).T
    return [columns[0:depth, s : s + 1] for s in range(8)]


def bcast(v):
    return jnp.broadcast_to(v, (8, LANES))


def inverse_factor(tiles, rows, lanes, m=8, g=4):
    size = 8 * len(tiles)
    tiles, out = list(tiles), [None] * len(tiles)

    def total(terms):
        while len(terms) > 1:
            terms = [sum(terms[z : z + 2]) for z in range(0, len(terms), 2)]
        return terms[0]

    for k in range(0, size, m):
        b, j = divmod(k, 8)
        r = [bcast(tiles[b][j + i : j + i + 1, :]) for i in range(m)]
        s = [[bcast(r[i][:, k + l : k + l + 1]) if l >= i else None for l in range(m)] for i in range(m)]
        r = [r[i] + jnp.where(lanes == k + i, 1.0, 0.0) for i in range(m)]
        inv = [None] * m
        for q in range(0, m, g):
            scale, roots = None, []
            for p in range(q, q + g):
                product = s[p][p] if scale is None else scale * s[p][p]
                root = lax.rsqrt(product)
                inv[p] = root if scale is None else root * scale
                roots.append(root)
                for i in range(p + 1, q + g):
                    for l in range(m - 1, i - 1, -1):
                        s[i][l] = s[p][p] * s[i][l] - s[p][i] * s[p][l]
                    r[i] = s[p][p] * r[i] - s[p][i] * r[p]
                scale = product
            for p in range(q, q + g):
                r[p] = r[p] * roots[p - q]
                for l in range(p + 1, m):
                    s[p][l] = s[p][l] * roots[p - q]
            for i in range(q + g, m):
                for l in range(i, m):
                    s[i][l] = s[i][l] - total([s[p][i] * s[p][l] for p in range(q, q + g)])
                r[i] = r[i] - total([s[p][i] * r[p] for p in range(q, q + g)])
        for i in range(m):
            w = jnp.where(lanes < k + i, r[i], jnp.where(lanes == k + i, inv[i], 0.0))
            out[b] = w if out[b] is None else jnp.where(rows == j + i, w, out[b])
        if k + m >= size:
            break
        y = [r[i] * inv[i] for i in range(m)]
        for i in range(m):
            for l in range(i + 1, m):
                s[i][l] = s[i][l] * inv[i]
        for l in range(m - 1, 0, -1):
            for i in range(l - 1, -1, -1):
                y[i] = y[i] - s[i][l] * y[l]
        for i in range(b, len(tiles)):
            if i == b and j + m >= 8:
                continue
            terms = []
            for q in range(m):
                c = bcast(tiles[i][:, k + q : k + q + 1])
                if i == b:
                    c = jnp.where(rows > j + m - 1, c, 0.0)
                terms.append(c * y[q])
            tiles[i] = tiles[i] - total(terms)
    return out


def dense_rows(x, depth):
    left = LANES - depth
    blocks = []
    for g in range(0, 8, 4):
        for b in range(3):
            blocks.append(x[(g + b) * depth : (g + b + 1) * depth])
            last = (g + 3) * depth + left * b
            blocks.append(x[last : last + left])
    return jnp.concatenate(blocks, axis=0)


def first_kernel(length_ref, mine_ref, sib_ref, out_ref, work):
    width = work.shape[0]
    each = mine_ref.shape[0] // 4
    depth = each - 16
    starts = range(0, 4 * each, each)
    x = jnp.concatenate([ref[k : k + depth, :] for ref in (mine_ref, sib_ref) for k in starts], axis=0)
    w = jnp.concatenate(slice_weights(length_ref, depth), axis=0)
    xf = x.astype(jnp.float32)
    xw = xf * w
    parts = split3(xw)
    whole = 8 * depth
    out_ref[0:whole, :] = dense_rows(jnp.concatenate(parts[:2], axis=1), depth)
    turned = x.T
    gram = sum(jnp.dot(turned, part, preferred_element_type=jnp.float32) for part in parts)
    sq_row = jnp.sum(xf * xw, axis=0, keepdims=True)
    sq_col = jnp.broadcast_to(sq_row, (8, width)).T[:, 0:1]
    tail = mine_ref[depth:each, :].astype(jnp.float32)
    noise = tail[0:1, :] + tail[1:2, :] + tail[2:3, :]
    i = lax.broadcasted_iota(jnp.int32, (width, width), 0)
    j = lax.broadcasted_iota(jnp.int32, (width, width), 1)
    work[...] = jnp.exp(-0.5 * (sq_col + sq_row - 2.0 * gram)) + jnp.where(i == j, noise, 0.0)
    both = jnp.concatenate([sq_row, noise], axis=1)
    row = lax.broadcasted_iota(jnp.int32, (16, 2 * width), 0)
    rest = jnp.zeros((16, 2 * width), jnp.float32)
    for k, part in enumerate(split3(both)):
        rest = jnp.where(row == k, part.astype(jnp.float32), rest)
    out_ref[whole + width :, :] = rest.astype(jnp.bfloat16)
    rows = lax.broadcasted_iota(jnp.int32, (8, LANES), 0)
    lanes = lax.broadcasted_iota(jnp.int32, (8, LANES), 1)
    tiles = [work[8 * t : 8 * t + 8, :] for t in range(width // 8)]
    inverse = jnp.concatenate(inverse_factor(tiles, rows, lanes), axis=0)
    out_ref[whole : whole + width, :] = jnp.concatenate(split2(inverse), axis=1)


def first_tile(lengths, mine, sib):
    width = mine.shape[1]
    whole = 2 * (mine.shape[0] - 64)
    return pl.pallas_call(
        first_kernel,
        out_shape=jax.ShapeDtypeStruct((whole + width + 16, 2 * width), jnp.bfloat16),
        in_specs=[VM] * 3,
        out_specs=VM,
        scratch_shapes=[pltpu.VMEM((width, width), jnp.float32)],
        name="first_tile",
    )(lengths, mine, sib)


def dense(refs, t, width, depth):
    left = LANES - depth
    lane = lax.broadcasted_iota(jnp.int32, (width, LANES), 1)
    blocks = []
    for g in range(0, 8, 4):
        if t < 3:
            parts = [ref[t * width : (t + 1) * width, :] for ref in refs[g : g + 4]]
            for b in range(3):
                moved = pltpu.roll(parts[3], depth - left * b, 1)
                blocks.append(jnp.where(lane < depth, parts[b], moved))
        else:
            for b in range(3):
                block = refs[g + 3][b * width : (b + 1) * width, :]
                for k in range(3):
                    moved = pltpu.roll(
                        refs[g + b][k * width : (k + 1) * width, :], LANES - depth + left * k, 1
                    )
                    block = jnp.where((lane >= left * k) & (lane < left * (k + 1)), moved, block)
                blocks.append(block)
    return jnp.concatenate(blocks, axis=1)


def dense_weights(length_ref, depth):
    parts = dense_rows(jnp.concatenate(slice_weights(length_ref, depth), axis=0), depth)
    return jnp.broadcast_to(parts, (8 * depth, LANES)).T[0:1, :]


def three(x):
    hi, lo = split2(x)
    return jnp.concatenate([hi, lo, hi], axis=1)


def twice(y):
    hi, lo = split2(y)
    return jnp.concatenate([hi, hi, lo], axis=1)


def rest_kernel(depth, length_ref, noise_ref, first_hbm, *refs):
    row_refs, col_refs, (panel_hbm, trail_hbm, first_ref, panel_ref, trail_ref, sems) = refs[:4], refs[4:8], refs[8:]
    width, whole = noise_ref.shape[1], 8 * depth
    copy = pltpu.make_async_copy(first_hbm, first_ref, sems.at[0])
    copy.start()
    h = 3 * width
    cut = lambda ref, k: ref.at[pl.ds(k * h, h)]
    cuts = lambda ref: [ref.at[pl.ds(k * h, h)] for k in range(ref.shape[0] // h)]
    row_own, row_oth = cuts(row_refs[0]) + cuts(row_refs[1]), cuts(row_refs[2]) + cuts(row_refs[3])
    cols = sum((cuts(ref) for ref in col_refs), [])
    row_id, col_id, n_rows = lax.axis_index("row"), lax.axis_index("col"), lax.axis_size("row")
    parity, on_diag = col_id // n_rows, row_id == col_id % n_rows

    w = dense_weights(length_ref, depth)
    blocks = w.shape[1] // LANES

    def squares(xf, xw):
        partial = xf[:, 0:LANES] * xw[:, 0:LANES]
        for s in range(1, blocks):
            cut = slice(s * LANES, (s + 1) * LANES)
            partial = partial + xf[:, cut] * xw[:, cut]
        return partial

    eye = lax.broadcasted_iota(jnp.int32, (width, width), 0) == lax.broadcasted_iota(
        jnp.int32, (width, width), 1
    )
    copy.wait()
    inv = first_ref[whole : whole + width, :]
    inv = jnp.concatenate([inv[:, 0:width], inv], axis=1)
    tail = first_ref[whole + width :, :].astype(jnp.float32)
    tail = tail[0:1, :] + tail[1:2, :] + tail[2:3, :]
    sq0, diag0 = tail[:, 0:width], jnp.where(eye, tail[:, width:], 0.0)

    def panel_of(x, sq, heads):
        gram = jnp.dot(x, first_ref[0:whole, :], preferred_element_type=jnp.float32)
        gram = gram[:, 0:width] + gram[:, width:]
        kern = jnp.exp(gram - 0.5 * (sq + sq0))
        if heads:
            tops = [
                kern[h * width : (h + 1) * width] + jnp.where(c, diag0, 0.0)
                for h, c in enumerate(heads)
            ]
            if len(heads) * width < kern.shape[0]:
                tops.append(kern[len(heads) * width :])
            kern = jnp.concatenate(tops, axis=0)
        return nt(three(kern), inv)

    c_hi, c_lo, c_sq, c_panel = [], [], [], []
    for t in range(4):
        c = dense(cols, t, width, depth)
        cf = c.astype(jnp.float32)
        cw = cf * w
        partial = squares(cf, cw)
        hi, lo = split2(cw)
        c_hi.append(hi)
        c_lo.append(lo)
        c_sq.append(jnp.sum(partial.T, axis=0, keepdims=True))
        sq = jnp.sum(partial, axis=1, keepdims=True)
        c_panel.append(panel_of(c, sq, [col_id == 0] if t == 0 else []))
    c_hi, c_lo = jnp.concatenate(c_hi, axis=0), jnp.concatenate(c_lo, axis=0)
    c_sq = jnp.concatenate(c_sq, axis=1)
    c_panel = twice(jnp.concatenate(c_panel, axis=0))

    outs = []
    for t in range(4):
        x = jnp.concatenate([dense(row_own, t, width, depth), dense(row_oth, t, width, depth)], axis=0)
        xf = x.astype(jnp.float32)
        sq = jnp.sum(squares(xf, xf * w), axis=1, keepdims=True)
        heads = [(row_id == 0) & (parity == h) for h in range(2)] if t == 0 else []
        panel = panel_of(x, sq, heads)
        gram = nt(x, c_hi) + nt(x, c_lo)
        kern = jnp.exp(gram - 0.5 * (sq + c_sq))
        trail = kern - nt(three(panel), c_panel)
        for half in range(2):
            tile = 2 * t + (parity if half == 0 else 1 - parity)
            low = half * width
            panel_ref[tile] = panel[low : low + width]
            for tc in range(4):
                block = trail[low : low + width, tc * width : (tc + 1) * width]
                if half == 0 and tc == t:
                    block = block + jnp.where(eye & on_diag, noise_ref[pl.ds(tile, 1), :], 0.0)
                trail_ref[pl.ds(tile * (4 * width) + tc, width, stride=4), :] = block
            span = pl.ds(tile * (4 * width), 4 * width)
            for n, (src, dst) in enumerate(
                ((panel_ref.at[tile], panel_hbm.at[tile]), (trail_ref.at[span], trail_hbm.at[span]))
            ):
                outs.append(pltpu.make_async_copy(src, dst, sems.at[1 + 4 * t + 2 * half + n]))
                outs[-1].start()
    for copy in outs:
        copy.wait()


def rest(depth, lengths, noise, first, *slices):
    tiles, width = noise.shape
    return pl.pallas_call(
        functools.partial(rest_kernel, depth),
        out_shape=(
            jax.ShapeDtypeStruct((tiles, width, width), jnp.float32),
            jax.ShapeDtypeStruct((tiles * width * 4, width), jnp.float32),
        ),
        in_specs=[VM] * 2 + [ANY] + [VM] * 8,
        out_specs=(ANY, ANY),
        scratch_shapes=[
            pltpu.VMEM(first.shape, first.dtype),
            pltpu.VMEM((tiles, width, width), jnp.float32),
            pltpu.VMEM((tiles * width * 4, width), jnp.float32),
            pltpu.SemaphoreType.DMA((17,)),
        ],
        compiler_params=pltpu.CompilerParams(vmem_limit_bytes=VMEM_REST * 1024 * 1024),
        name="rest",
    )(lengths, noise, first, *slices)


def body(features, lengthscale, noise):
    tiles, width, depth = features.shape
    row_id = lax.axis_index("row")
    col_id = lax.axis_index("col")
    n_rows, n_cols = lax.axis_size("row"), lax.axis_size("col")
    home = col_id % n_rows
    parity = col_id // n_rows

    def over_row(x, k):
        return lax.ppermute(x, "row", [(i, i ^ k) for i in range(n_rows)])

    def over_col(x, k):
        return lax.ppermute(x, "col", [(i, i ^ k) for i in range(n_cols)])

    feats = jnp.transpose(features, (0, 2, 1))
    lengths = lengthscale.reshape(-1, LANES)

    def after(x, *others):
        return lax.optimization_barrier((x, *others))[0]

    own, oth, own_long, oth_long = pack(feats, noise)
    size = own.shape[0]
    near, p2, p3 = over_col(own, 2), over_col(oth, 4), over_col(oth, 6)
    first_planes = [own_long] + [over_row(own_long, k) for k in (1, 2, 3)]
    head = lax.select_n(row_id, *[v[size:] for v in first_planes])
    q1 = over_col(lax.dynamic_update_slice(oth_long, head, (size, 0)), 2)
    half = lax.dynamic_update_slice(own_long, head, (size, 0))
    q2, q3 = over_col(half, 4), over_col(half, 6)
    p = jnp.concatenate([near, p2, p3], axis=0)
    planes = [p] + [over_row(p, k) for k in (1, 2, 3)]
    p = jnp.concatenate([own, near, p2, p3], axis=0)
    stack = jnp.concatenate([head] + [v[size:] for v in (q1, q2, q3)], axis=0)
    first = first_tile(lengths, stack, over_col(stack, 1))
    q = jnp.concatenate([oth] + [v[:size] for v in (q1, q2, q3)], axis=0)
    sibs = [over_col(v, 1) for v in (p, q)]
    *planes, _ = lax.optimization_barrier((*planes, first))
    first_planes = [v[:size] for v in first_planes]
    keep = [lax.select_n(row_id ^ home, *v) for v in (first_planes, planes)]
    give = [over_col(lax.select_n(row_id ^ home ^ 1, *v), 1) for v in (first_planes, planes)]
    panel, trailing = rest(depth, lengths, noise, first, p, sibs[0], q, sibs[1], *keep, *give)
    return panel, trailing.reshape(tiles, width, 4, width)


def from_root(block, axis, holder):
    block = jnp.where(lax.axis_index(axis) == holder, block, jnp.zeros_like(block))
    return lax.psum(block, axis)


def general_body(features, lengthscale, noise):
    rows_axis = lax.axis_size("row")
    cols_axis = lax.axis_size("col")
    row_id = lax.axis_index("row")
    col_id = lax.axis_index("col")
    tiles_row = features.shape[0]
    width = features.shape[1]
    stride = cols_axis // rows_axis
    tiles_col = tiles_row // stride
    row_feats = lax.all_gather(features, "col", axis=2, tiled=True)
    depth = row_feats.shape[2]
    grouped = row_feats.reshape(tiles_col, stride, width, depth)
    picked = lax.dynamic_index_in_dim(grouped, col_id // rows_axis, 1, keepdims=False)
    col_feats = from_root(picked, "row", col_id % rows_axis)
    inverse = 1.0 / lengthscale
    left = row_feats.reshape(tiles_row * width, depth).astype(jnp.float32) * inverse[None, :]
    right = col_feats.reshape(tiles_col * width, depth).astype(jnp.float32) * inverse[None, :]
    left_sq = jnp.sum(left * left, axis=1)
    right_sq = jnp.sum(right * right, axis=1)
    inner = jnp.arange(width, dtype=jnp.int32)
    row_index = (
        (jnp.arange(tiles_row, dtype=jnp.int32)[:, None] * rows_axis + row_id) * width + inner[None, :]
    ).reshape(-1)
    col_index = (
        (jnp.arange(tiles_col, dtype=jnp.int32)[:, None] * cols_axis + col_id) * width + inner[None, :]
    ).reshape(-1)
    gram = jnp.dot(left, right.T, precision=lax.Precision.HIGHEST)
    kern = jnp.exp(-0.5 * (left_sq[:, None] + right_sq[None, :] - 2.0 * gram))
    kern = kern + jnp.where(row_index[:, None] == col_index[None, :], noise.reshape(-1)[:, None], 0.0)
    diag_tile = from_root(kern[:width, :width], "row", 0)
    factor = jnp.linalg.cholesky(diag_tile)
    own_rows = jax.scipy.linalg.solve_triangular(factor, kern[:, :width].T, lower=True).T
    panel_rows = from_root(own_rows, "col", 0)
    panel_grouped = panel_rows.reshape(tiles_col, stride, width, width)
    panel_pick = lax.dynamic_index_in_dim(panel_grouped, col_id // rows_axis, 1, keepdims=False)
    panel_cols = from_root(panel_pick, "row", col_id % rows_axis).reshape(tiles_col * width, width)
    trailing = kern - jnp.dot(panel_rows, panel_cols.T, precision=lax.Precision.HIGHEST)
    return (
        panel_rows.reshape(tiles_row, width, width),
        trailing.reshape(tiles_row, width, tiles_col, width),
    )


def solution(mesh):
    placed = (P(None, "row", "col"), P(), P(None, "row"))
    small = mesh.shape["row"] == 4 and mesh.shape["col"] == 8
    return jax.shard_map(
        body if small else general_body,
        mesh=mesh,
        in_specs=placed,
        out_specs=(P(None, "row", None), P(None, "row", None, "col")),
        check_vma=False,
    )
```

```python
import functools

import jax
import jax.numpy as jnp
from jax import lax
from jax.experimental import pallas as pl
from jax.experimental.pallas import tpu as pltpu
from jax.sharding import PartitionSpec as P

LANES = 128
VMEM_REST = 32
ORDER = (0, 2, 4, 6, 1, 3, 5, 7)
VM = pl.BlockSpec(memory_space=pltpu.VMEM)
ANY = pl.BlockSpec(memory_space=pl.ANY)


def nt(a, b, precision=None):
    return lax.dot_general(
        a, b, (((1,), (1,)), ((), ())), precision=precision, preferred_element_type=jnp.float32
    )


def split2(x):
    hi = x.astype(jnp.bfloat16)
    return hi, (x - hi.astype(jnp.float32)).astype(jnp.bfloat16)


def split3(x):
    hi, mid = split2(x)
    rest = x - hi.astype(jnp.float32) - mid.astype(jnp.float32)
    return hi, mid, rest.astype(jnp.bfloat16)


def pack_kernel(feat_ref, noise_ref, own_ref, oth_ref, own_long_ref, oth_long_ref):
    tiles, depth, width = feat_ref.shape
    left = LANES - depth
    parity = lax.axis_index("col") // lax.axis_size("row")
    for half, outs in ((0, (own_ref, own_long_ref)), (1, (oth_ref, oth_long_ref))):
        tile = [feat_ref[2 * k + (parity if half == 0 else 1 - parity)] for k in range(4)]
        for k in range(3):
            block = jnp.concatenate([tile[k], tile[3][left * k : left * (k + 1)]], axis=0).T
            for out_ref in outs:
                out_ref[k * width : (k + 1) * width, :] = block
    row = lax.broadcasted_iota(jnp.int32, (16, width), 0)
    parts = jnp.zeros((16, width), jnp.float32)
    for k, part in enumerate(split3(noise_ref[0:1, :])):
        parts = jnp.where(row == k, part.astype(jnp.float32), parts)
    for out_ref in (own_long_ref, oth_long_ref):
        out_ref[3 * width : 3 * width + depth, :] = feat_ref[0]
        out_ref[3 * width + depth :, :] = parts.astype(jnp.bfloat16)


def pack(feats, noise):
    _, depth, width = feats.shape
    rows = lambda n: jax.ShapeDtypeStruct((n, width), jnp.bfloat16)
    return pl.pallas_call(
        pack_kernel,
        out_shape=(
            rows(3 * width),
            rows(3 * width),
            rows(3 * width + depth + 16),
            rows(3 * width + depth + 16),
        ),
        in_specs=[VM, VM],
        out_specs=(VM,) * 4,
        name="pack",
    )(feats, noise)


def slice_weights(length_ref, depth):
    col_id = lax.axis_index("col")
    lane = lax.broadcasted_iota(jnp.int32, (8, LANES), 1)
    row = lax.broadcasted_iota(jnp.int32, (8, LANES), 0)
    held = jnp.ones((8, LANES), jnp.float32)
    for s in range(8):
        chunk, off = divmod(depth * s, LANES)
        here = jnp.broadcast_to(length_ref[chunk : chunk + 1, :], (8, LANES))
        if off:
            here = pltpu.roll(here, LANES - off, 1)
        if off + depth > LANES:
            more = jnp.broadcast_to(length_ref[chunk + 1 : chunk + 2, :], (8, LANES))
            here = jnp.where(lane < LANES - off, here, pltpu.roll(more, LANES - off, 1))
        for place, k in enumerate(ORDER):
            held = jnp.where((row == place) & (col_id == (s ^ k)), here, held)
    inverse = 1.0 / held
    columns = (inverse * inverse).T
    return [columns[0:depth, s : s + 1] for s in range(8)]


def bcast(v):
    return jnp.broadcast_to(v, (8, LANES))


def inverse_factor(tiles, rows, lanes, m=8, g=4):
    size = 8 * len(tiles)
    tiles, out = list(tiles), [None] * len(tiles)

    def total(terms):
        while len(terms) > 1:
            terms = [sum(terms[z : z + 2]) for z in range(0, len(terms), 2)]
        return terms[0]

    for k in range(0, size, m):
        b, j = divmod(k, 8)
        r = [bcast(tiles[b][j + i : j + i + 1, :]) for i in range(m)]
        s = [[bcast(r[i][:, k + l : k + l + 1]) if l >= i else None for l in range(m)] for i in range(m)]
        r = [r[i] + jnp.where(lanes == k + i, 1.0, 0.0) for i in range(m)]
        inv = [None] * m
        for q in range(0, m, g):
            scale, roots = None, []
            for p in range(q, q + g):
                product = s[p][p] if scale is None else scale * s[p][p]
                root = lax.rsqrt(product)
                inv[p] = root if scale is None else root * scale
                roots.append(root)
                for i in range(p + 1, q + g):
                    for l in range(m - 1, i - 1, -1):
                        s[i][l] = s[p][p] * s[i][l] - s[p][i] * s[p][l]
                    r[i] = s[p][p] * r[i] - s[p][i] * r[p]
                scale = product
            for p in range(q, q + g):
                r[p] = r[p] * roots[p - q]
                for l in range(p + 1, m):
                    s[p][l] = s[p][l] * roots[p - q]
            for i in range(q + g, m):
                for l in range(i, m):
                    s[i][l] = s[i][l] - total([s[p][i] * s[p][l] for p in range(q, q + g)])
                r[i] = r[i] - total([s[p][i] * r[p] for p in range(q, q + g)])
        for i in range(m):
            w = jnp.where(lanes < k + i, r[i], jnp.where(lanes == k + i, inv[i], 0.0))
            out[b] = w if out[b] is None else jnp.where(rows == j + i, w, out[b])
        if k + m >= size:
            break
        y = [r[i] * inv[i] for i in range(m)]
        for i in range(m):
            for l in range(i + 1, m):
                s[i][l] = s[i][l] * inv[i]
        for l in range(m - 1, 0, -1):
            for i in range(l - 1, -1, -1):
                y[i] = y[i] - s[i][l] * y[l]
        for i in range(b, len(tiles)):
            if i == b and j + m >= 8:
                continue
            terms = []
            for q in range(m):
                c = bcast(tiles[i][:, k + q : k + q + 1])
                if i == b:
                    c = jnp.where(rows > j + m - 1, c, 0.0)
                terms.append(c * y[q])
            tiles[i] = tiles[i] - total(terms)
    return out


def dense_rows(x, depth):
    left = LANES - depth
    blocks = []
    for g in range(0, 8, 4):
        for b in range(3):
            blocks.append(x[(g + b) * depth : (g + b + 1) * depth])
            last = (g + 3) * depth + left * b
            blocks.append(x[last : last + left])
    return jnp.concatenate(blocks, axis=0)


def first_kernel(length_ref, mine_ref, sib_ref, out_ref, work):
    width = work.shape[0]
    each = mine_ref.shape[0] // 4
    depth = each - 16
    starts = range(0, 4 * each, each)
    x = jnp.concatenate([ref[k : k + depth, :] for ref in (mine_ref, sib_ref) for k in starts], axis=0)
    w = jnp.concatenate(slice_weights(length_ref, depth), axis=0)
    xf = x.astype(jnp.float32)
    xw = xf * w
    parts = split3(xw)
    whole = 8 * depth
    out_ref[0:whole, :] = dense_rows(jnp.concatenate(parts[:2], axis=1), depth)
    turned = x.T
    gram = sum(jnp.dot(turned, part, preferred_element_type=jnp.float32) for part in parts)
    sq_row = jnp.sum(xf * xw, axis=0, keepdims=True)
    sq_col = jnp.broadcast_to(sq_row, (8, width)).T[:, 0:1]
    tail = mine_ref[depth:each, :].astype(jnp.float32)
    noise = tail[0:1, :] + tail[1:2, :] + tail[2:3, :]
    i = lax.broadcasted_iota(jnp.int32, (width, width), 0)
    j = lax.broadcasted_iota(jnp.int32, (width, width), 1)
    work[...] = jnp.exp(-0.5 * (sq_col + sq_row - 2.0 * gram)) + jnp.where(i == j, noise, 0.0)
    both = jnp.concatenate([sq_row, noise], axis=1)
    row = lax.broadcasted_iota(jnp.int32, (16, 2 * width), 0)
    rest = jnp.zeros((16, 2 * width), jnp.float32)
    for k, part in enumerate(split3(both)):
        rest = jnp.where(row == k, part.astype(jnp.float32), rest)
    out_ref[whole + width :, :] = rest.astype(jnp.bfloat16)
    rows = lax.broadcasted_iota(jnp.int32, (8, LANES), 0)
    lanes = lax.broadcasted_iota(jnp.int32, (8, LANES), 1)
    tiles = [work[8 * t : 8 * t + 8, :] for t in range(width // 8)]
    inverse = jnp.concatenate(inverse_factor(tiles, rows, lanes), axis=0)
    out_ref[whole : whole + width, :] = jnp.concatenate(split2(inverse), axis=1)


def first_tile(lengths, mine, sib):
    width = mine.shape[1]
    whole = 2 * (mine.shape[0] - 64)
    return pl.pallas_call(
        first_kernel,
        out_shape=jax.ShapeDtypeStruct((whole + width + 16, 2 * width), jnp.bfloat16),
        in_specs=[VM] * 3,
        out_specs=VM,
        scratch_shapes=[pltpu.VMEM((width, width), jnp.float32)],
        name="first_tile",
    )(lengths, mine, sib)


def dense(refs, t, width, depth):
    left = LANES - depth
    lane = lax.broadcasted_iota(jnp.int32, (width, LANES), 1)
    blocks = []
    for g in range(0, 8, 4):
        if t < 3:
            parts = [ref[t * width : (t + 1) * width, :] for ref in refs[g : g + 4]]
            for b in range(3):
                moved = pltpu.roll(parts[3], depth - left * b, 1)
                blocks.append(jnp.where(lane < depth, parts[b], moved))
        else:
            for b in range(3):
                block = refs[g + 3][b * width : (b + 1) * width, :]
                for k in range(3):
                    moved = pltpu.roll(
                        refs[g + b][k * width : (k + 1) * width, :], LANES - depth + left * k, 1
                    )
                    block = jnp.where((lane >= left * k) & (lane < left * (k + 1)), moved, block)
                blocks.append(block)
    return jnp.concatenate(blocks, axis=1)


def dense_weights(length_ref, depth):
    parts = dense_rows(jnp.concatenate(slice_weights(length_ref, depth), axis=0), depth)
    return jnp.broadcast_to(parts, (8 * depth, LANES)).T[0:1, :]


def three(x):
    hi, lo = split2(x)
    return jnp.concatenate([hi, lo, hi], axis=1)


def twice(y):
    hi, lo = split2(y)
    return jnp.concatenate([hi, hi, lo], axis=1)


def rest_kernel(depth, length_ref, noise_ref, first_hbm, *refs):
    row_refs, col_refs, (panel_hbm, trail_hbm, first_ref, panel_ref, trail_ref, sems) = refs[:4], refs[4:8], refs[8:]
    width, whole = noise_ref.shape[1], 8 * depth
    copy = pltpu.make_async_copy(first_hbm, first_ref, sems.at[0])
    copy.start()
    h = 3 * width
    cut = lambda ref, k: ref.at[pl.ds(k * h, h)]
    cuts = lambda ref: [ref.at[pl.ds(k * h, h)] for k in range(ref.shape[0] // h)]
    row_own, row_oth = cuts(row_refs[0]) + cuts(row_refs[1]), cuts(row_refs[2]) + cuts(row_refs[3])
    cols = sum((cuts(ref) for ref in col_refs), [])
    row_id, col_id, n_rows = lax.axis_index("row"), lax.axis_index("col"), lax.axis_size("row")
    parity, on_diag = col_id // n_rows, row_id == col_id % n_rows

    w = dense_weights(length_ref, depth)
    blocks = w.shape[1] // LANES

    def squares(xf, xw):
        partial = xf[:, 0:LANES] * xw[:, 0:LANES]
        for s in range(1, blocks):
            cut = slice(s * LANES, (s + 1) * LANES)
            partial = partial + xf[:, cut] * xw[:, cut]
        return partial

    eye = lax.broadcasted_iota(jnp.int32, (width, width), 0) == lax.broadcasted_iota(
        jnp.int32, (width, width), 1
    )
    copy.wait()
    inv = first_ref[whole : whole + width, :]
    inv = jnp.concatenate([inv[:, 0:width], inv], axis=1)
    tail = first_ref[whole + width :, :].astype(jnp.float32)
    tail = tail[0:1, :] + tail[1:2, :] + tail[2:3, :]
    sq0, diag0 = tail[:, 0:width], jnp.where(eye, tail[:, width:], 0.0)

    def kern_of(x, sq, heads):
        gram = jnp.dot(x, first_ref[0:whole, :], preferred_element_type=jnp.float32)
        gram = gram[:, 0:width] + gram[:, width:]
        kern = jnp.exp(gram - 0.5 * (sq + sq0))
        if heads:
            tops = [
                kern[h * width : (h + 1) * width] + jnp.where(c, diag0, 0.0)
                for h, c in enumerate(heads)
            ]
            if len(heads) * width < kern.shape[0]:
                tops.append(kern[len(heads) * width :])
            kern = jnp.concatenate(tops, axis=0)
        return kern

    c_hi, c_lo, c_sq, c_panel = [], [], [], []
    for t in range(4):
        c = dense(cols, t, width, depth)
        cf = c.astype(jnp.float32)
        cw = cf * w
        partial = squares(cf, cw)
        hi, lo = split2(cw)
        c_hi.append(hi)
        c_lo.append(lo)
        c_sq.append(jnp.sum(partial.T, axis=0, keepdims=True))
        sq = jnp.sum(partial, axis=1, keepdims=True)
        c_panel.append(kern_of(c, sq, [col_id == 0] if t == 0 else []))
    c_hi, c_lo = jnp.concatenate(c_hi, axis=0), jnp.concatenate(c_lo, axis=0)
    c_sq = jnp.concatenate(c_sq, axis=1)
    c_panel = twice(nt(three(jnp.concatenate(c_panel, axis=0)), inv))

    outs, xs, sqs, kerns = [], [], [], []
    for t in range(4):
        x = jnp.concatenate([dense(row_own, t, width, depth), dense(row_oth, t, width, depth)], axis=0)
        xf = x.astype(jnp.float32)
        sq = jnp.sum(squares(xf, xf * w), axis=1, keepdims=True)
        heads = [(row_id == 0) & (parity == h) for h in range(2)] if t == 0 else []
        xs.append(x)
        sqs.append(sq)
        kerns.append(kern_of(x, sq, heads))
    parts = []
    for t in range(4):
        panel = nt(three(kerns[t]), inv)
        parts.append(three(panel))
        for half in range(2):
            tile = 2 * t + (parity if half == 0 else 1 - parity)
            panel_ref[tile] = panel[half * width : (half + 1) * width]
            outs.append(pltpu.make_async_copy(panel_ref.at[tile], panel_hbm.at[tile], sems.at[1 + 2 * t + half]))
            outs[-1].start()
    for t in range(4):
        gram = nt(xs[t], c_hi) + nt(xs[t], c_lo)
        update = nt(parts[t], c_panel)
        trail = jnp.exp(gram - 0.5 * (sqs[t] + c_sq)) - update
        for half in range(2):
            tile = 2 * t + (parity if half == 0 else 1 - parity)
            low = half * width
            for tc in range(4):
                block = trail[low : low + width, tc * width : (tc + 1) * width]
                if half == 0 and tc == t:
                    block = block + jnp.where(eye & on_diag, noise_ref[pl.ds(tile, 1), :], 0.0)
                trail_ref[pl.ds(tile * (4 * width) + tc, width, stride=4), :] = block
            span = pl.ds(tile * (4 * width), 4 * width)
            outs.append(pltpu.make_async_copy(trail_ref.at[span], trail_hbm.at[span], sems.at[9 + 2 * t + half]))
            outs[-1].start()
    for copy in outs:
        copy.wait()


def rest(depth, lengths, noise, first, *slices):
    tiles, width = noise.shape
    return pl.pallas_call(
        functools.partial(rest_kernel, depth),
        out_shape=(
            jax.ShapeDtypeStruct((tiles, width, width), jnp.float32),
            jax.ShapeDtypeStruct((tiles * width * 4, width), jnp.float32),
        ),
        in_specs=[VM] * 2 + [ANY] + [VM] * 8,
        out_specs=(ANY, ANY),
        scratch_shapes=[
            pltpu.VMEM(first.shape, first.dtype),
            pltpu.VMEM((tiles, width, width), jnp.float32),
            pltpu.VMEM((tiles * width * 4, width), jnp.float32),
            pltpu.SemaphoreType.DMA((17,)),
        ],
        compiler_params=pltpu.CompilerParams(vmem_limit_bytes=VMEM_REST * 1024 * 1024),
        name="rest",
    )(lengths, noise, first, *slices)


def body(features, lengthscale, noise):
    tiles, width, depth = features.shape
    row_id = lax.axis_index("row")
    col_id = lax.axis_index("col")
    n_rows, n_cols = lax.axis_size("row"), lax.axis_size("col")
    home = col_id % n_rows
    parity = col_id // n_rows

    def over_row(x, k):
        return lax.ppermute(x, "row", [(i, i ^ k) for i in range(n_rows)])

    def over_col(x, k):
        return lax.ppermute(x, "col", [(i, i ^ k) for i in range(n_cols)])

    feats = jnp.transpose(features, (0, 2, 1))
    lengths = lengthscale.reshape(-1, LANES)

    def after(x, *others):
        return lax.optimization_barrier((x, *others))[0]

    own, oth, own_long, oth_long = pack(feats, noise)
    size = own.shape[0]
    near, p2, p3 = over_col(own, 2), over_col(oth, 4), over_col(oth, 6)
    first_planes = [own_long] + [over_row(own_long, k) for k in (1, 2, 3)]
    head = lax.select_n(row_id, *[v[size:] for v in first_planes])
    q1 = over_col(lax.dynamic_update_slice(oth_long, head, (size, 0)), 2)
    half = lax.dynamic_update_slice(own_long, head, (size, 0))
    q2, q3 = over_col(half, 4), over_col(half, 6)
    p = jnp.concatenate([near, p2, p3], axis=0)
    planes = [p] + [over_row(p, k) for k in (1, 2, 3)]
    p = jnp.concatenate([own, near, p2, p3], axis=0)
    stack = jnp.concatenate([head] + [v[size:] for v in (q1, q2, q3)], axis=0)
    first = first_tile(lengths, stack, over_col(stack, 1))
    q = jnp.concatenate([oth] + [v[:size] for v in (q1, q2, q3)], axis=0)
    sibs = [over_col(v, 1) for v in (p, q)]
    *planes, _ = lax.optimization_barrier((*planes, first))
    first_planes = [v[:size] for v in first_planes]
    keep = [lax.select_n(row_id ^ home, *v) for v in (first_planes, planes)]
    give = [over_col(lax.select_n(row_id ^ home ^ 1, *v), 1) for v in (first_planes, planes)]
    panel, trailing = rest(depth, lengths, noise, first, p, sibs[0], q, sibs[1], *keep, *give)
    return panel, trailing.reshape(tiles, width, 4, width)


def from_root(block, axis, holder):
    block = jnp.where(lax.axis_index(axis) == holder, block, jnp.zeros_like(block))
    return lax.psum(block, axis)


def general_body(features, lengthscale, noise):
    rows_axis = lax.axis_size("row")
    cols_axis = lax.axis_size("col")
    row_id = lax.axis_index("row")
    col_id = lax.axis_index("col")
    tiles_row = features.shape[0]
    width = features.shape[1]
    stride = cols_axis // rows_axis
    tiles_col = tiles_row // stride
    row_feats = lax.all_gather(features, "col", axis=2, tiled=True)
    depth = row_feats.shape[2]
    grouped = row_feats.reshape(tiles_col, stride, width, depth)
    picked = lax.dynamic_index_in_dim(grouped, col_id // rows_axis, 1, keepdims=False)
    col_feats = from_root(picked, "row", col_id % rows_axis)
    inverse = 1.0 / lengthscale
    left = row_feats.reshape(tiles_row * width, depth).astype(jnp.float32) * inverse[None, :]
    right = col_feats.reshape(tiles_col * width, depth).astype(jnp.float32) * inverse[None, :]
    left_sq = jnp.sum(left * left, axis=1)
    right_sq = jnp.sum(right * right, axis=1)
    inner = jnp.arange(width, dtype=jnp.int32)
    row_index = (
        (jnp.arange(tiles_row, dtype=jnp.int32)[:, None] * rows_axis + row_id) * width + inner[None, :]
    ).reshape(-1)
    col_index = (
        (jnp.arange(tiles_col, dtype=jnp.int32)[:, None] * cols_axis + col_id) * width + inner[None, :]
    ).reshape(-1)
    gram = jnp.dot(left, right.T, precision=lax.Precision.HIGHEST)
    kern = jnp.exp(-0.5 * (left_sq[:, None] + right_sq[None, :] - 2.0 * gram))
    kern = kern + jnp.where(row_index[:, None] == col_index[None, :], noise.reshape(-1)[:, None], 0.0)
    diag_tile = from_root(kern[:width, :width], "row", 0)
    factor = jnp.linalg.cholesky(diag_tile)
    own_rows = jax.scipy.linalg.solve_triangular(factor, kern[:, :width].T, lower=True).T
    panel_rows = from_root(own_rows, "col", 0)
    panel_grouped = panel_rows.reshape(tiles_col, stride, width, width)
    panel_pick = lax.dynamic_index_in_dim(panel_grouped, col_id // rows_axis, 1, keepdims=False)
    panel_cols = from_root(panel_pick, "row", col_id % rows_axis).reshape(tiles_col * width, width)
    trailing = kern - jnp.dot(panel_rows, panel_cols.T, precision=lax.Precision.HIGHEST)
    return (
        panel_rows.reshape(tiles_row, width, width),
        trailing.reshape(tiles_row, width, tiles_col, width),
    )


def solution(mesh):
    placed = (P(None, "row", "col"), P(), P(None, "row"))
    small = mesh.shape["row"] == 4 and mesh.shape["col"] == 8
    return jax.shard_map(
        body if small else general_body,
        mesh=mesh,
        in_specs=placed,
        out_specs=(P(None, "row", None), P(None, "row", None, "col")),
        check_vma=False,
    )
```

```python
import functools

import jax
import jax.numpy as jnp
from jax import lax
from jax.experimental import pallas as pl
from jax.experimental.pallas import tpu as pltpu
from jax.sharding import PartitionSpec as P

LANES = 128
VMEM_REST = 32
ORDER = (0, 2, 4, 6, 1, 3, 5, 7)
VM = pl.BlockSpec(memory_space=pltpu.VMEM)
ANY = pl.BlockSpec(memory_space=pl.ANY)


def nt(a, b, precision=None):
    return lax.dot_general(
        a, b, (((1,), (1,)), ((), ())), precision=precision, preferred_element_type=jnp.float32
    )


def split2(x):
    hi = x.astype(jnp.bfloat16)
    return hi, (x - hi.astype(jnp.float32)).astype(jnp.bfloat16)


def split3(x):
    hi, mid = split2(x)
    rest = x - hi.astype(jnp.float32) - mid.astype(jnp.float32)
    return hi, mid, rest.astype(jnp.bfloat16)


def pack_kernel(feat_ref, noise_ref, own_ref, oth_ref, own_long_ref, oth_long_ref):
    tiles, depth, width = feat_ref.shape
    left = LANES - depth
    parity = lax.axis_index("col") // lax.axis_size("row")
    for half, outs in ((0, (own_ref, own_long_ref)), (1, (oth_ref, oth_long_ref))):
        tile = [feat_ref[2 * k + (parity if half == 0 else 1 - parity)] for k in range(4)]
        for k in range(3):
            block = jnp.concatenate([tile[k], tile[3][left * k : left * (k + 1)]], axis=0).T
            for out_ref in outs:
                out_ref[k * width : (k + 1) * width, :] = block
    row = lax.broadcasted_iota(jnp.int32, (16, width), 0)
    parts = jnp.zeros((16, width), jnp.float32)
    for k, part in enumerate(split3(noise_ref[0:1, :])):
        parts = jnp.where(row == k, part.astype(jnp.float32), parts)
    for out_ref in (own_long_ref, oth_long_ref):
        out_ref[3 * width : 3 * width + depth, :] = feat_ref[0]
        out_ref[3 * width + depth :, :] = parts.astype(jnp.bfloat16)


def pack(feats, noise):
    _, depth, width = feats.shape
    rows = lambda n: jax.ShapeDtypeStruct((n, width), jnp.bfloat16)
    return pl.pallas_call(
        pack_kernel,
        out_shape=(
            rows(3 * width),
            rows(3 * width),
            rows(3 * width + depth + 16),
            rows(3 * width + depth + 16),
        ),
        in_specs=[VM, VM],
        out_specs=(VM,) * 4,
        name="pack",
    )(feats, noise)


def slice_weights(length_ref, depth):
    col_id = lax.axis_index("col")
    lane = lax.broadcasted_iota(jnp.int32, (8, LANES), 1)
    row = lax.broadcasted_iota(jnp.int32, (8, LANES), 0)
    held = jnp.ones((8, LANES), jnp.float32)
    for s in range(8):
        chunk, off = divmod(depth * s, LANES)
        here = jnp.broadcast_to(length_ref[chunk : chunk + 1, :], (8, LANES))
        if off:
            here = pltpu.roll(here, LANES - off, 1)
        if off + depth > LANES:
            more = jnp.broadcast_to(length_ref[chunk + 1 : chunk + 2, :], (8, LANES))
            here = jnp.where(lane < LANES - off, here, pltpu.roll(more, LANES - off, 1))
        for place, k in enumerate(ORDER):
            held = jnp.where((row == place) & (col_id == (s ^ k)), here, held)
    inverse = 1.0 / held
    columns = (inverse * inverse).T
    return [columns[0:depth, s : s + 1] for s in range(8)]


def bcast(v):
    return jnp.broadcast_to(v, (8, LANES))


def inverse_factor(tiles, rows, lanes, m=8, g=4):
    size = 8 * len(tiles)
    tiles, out = list(tiles), [None] * len(tiles)

    def total(terms):
        while len(terms) > 1:
            terms = [sum(terms[z : z + 2]) for z in range(0, len(terms), 2)]
        return terms[0]

    for k in range(0, size, m):
        b, j = divmod(k, 8)
        r = [bcast(tiles[b][j + i : j + i + 1, :]) for i in range(m)]
        s = [[bcast(r[i][:, k + l : k + l + 1]) if l >= i else None for l in range(m)] for i in range(m)]
        r = [r[i] + jnp.where(lanes == k + i, 1.0, 0.0) for i in range(m)]
        inv = [None] * m
        for q in range(0, m, g):
            scale, roots = None, []
            for p in range(q, q + g):
                product = s[p][p] if scale is None else scale * s[p][p]
                root = lax.rsqrt(product)
                inv[p] = root if scale is None else root * scale
                roots.append(root)
                for i in range(p + 1, q + g):
                    for l in range(m - 1, i - 1, -1):
                        s[i][l] = s[p][p] * s[i][l] - s[p][i] * s[p][l]
                    r[i] = s[p][p] * r[i] - s[p][i] * r[p]
                scale = product
            for p in range(q, q + g):
                r[p] = r[p] * roots[p - q]
                for l in range(p + 1, m):
                    s[p][l] = s[p][l] * roots[p - q]
            for i in range(q + g, m):
                for l in range(i, m):
                    s[i][l] = s[i][l] - total([s[p][i] * s[p][l] for p in range(q, q + g)])
                r[i] = r[i] - total([s[p][i] * r[p] for p in range(q, q + g)])
        for i in range(m):
            w = jnp.where(lanes < k + i, r[i], jnp.where(lanes == k + i, inv[i], 0.0))
            out[b] = w if out[b] is None else jnp.where(rows == j + i, w, out[b])
        if k + m >= size:
            break
        y = [r[i] * inv[i] for i in range(m)]
        for i in range(m):
            for l in range(i + 1, m):
                s[i][l] = s[i][l] * inv[i]
        for l in range(m - 1, 0, -1):
            for i in range(l - 1, -1, -1):
                y[i] = y[i] - s[i][l] * y[l]
        for i in range(b, len(tiles)):
            if i == b and j + m >= 8:
                continue
            terms = []
            for q in range(m):
                c = bcast(tiles[i][:, k + q : k + q + 1])
                if i == b:
                    c = jnp.where(rows > j + m - 1, c, 0.0)
                terms.append(c * y[q])
            tiles[i] = tiles[i] - total(terms)
    return out


def dense_rows(x, depth):
    left = LANES - depth
    blocks = []
    for g in range(0, 8, 4):
        for b in range(3):
            blocks.append(x[(g + b) * depth : (g + b + 1) * depth])
            last = (g + 3) * depth + left * b
            blocks.append(x[last : last + left])
    return jnp.concatenate(blocks, axis=0)


def first_kernel(length_ref, mine_ref, sib_ref, out_ref, work):
    width = work.shape[0]
    each = mine_ref.shape[0] // 4
    depth = each - 16
    starts = range(0, 4 * each, each)
    x = jnp.concatenate([ref[k : k + depth, :] for ref in (mine_ref, sib_ref) for k in starts], axis=0)
    w = jnp.concatenate(slice_weights(length_ref, depth), axis=0)
    xf = x.astype(jnp.float32)
    xw = xf * w
    parts = split3(xw)
    whole = 8 * depth
    out_ref[0:whole, :] = dense_rows(jnp.concatenate(parts[:2], axis=1), depth)
    turned = x.T
    gram = sum(jnp.dot(turned, part, preferred_element_type=jnp.float32) for part in parts)
    sq_row = jnp.sum(xf * xw, axis=0, keepdims=True)
    sq_col = jnp.broadcast_to(sq_row, (8, width)).T[:, 0:1]
    tail = mine_ref[depth:each, :].astype(jnp.float32)
    noise = tail[0:1, :] + tail[1:2, :] + tail[2:3, :]
    i = lax.broadcasted_iota(jnp.int32, (width, width), 0)
    j = lax.broadcasted_iota(jnp.int32, (width, width), 1)
    work[...] = jnp.exp(-0.5 * (sq_col + sq_row - 2.0 * gram)) + jnp.where(i == j, noise, 0.0)
    both = jnp.concatenate([sq_row, noise], axis=1)
    row = lax.broadcasted_iota(jnp.int32, (16, 2 * width), 0)
    rest = jnp.zeros((16, 2 * width), jnp.float32)
    for k, part in enumerate(split3(both)):
        rest = jnp.where(row == k, part.astype(jnp.float32), rest)
    out_ref[whole + width :, :] = rest.astype(jnp.bfloat16)
    rows = lax.broadcasted_iota(jnp.int32, (8, LANES), 0)
    lanes = lax.broadcasted_iota(jnp.int32, (8, LANES), 1)
    tiles = [work[8 * t : 8 * t + 8, :] for t in range(width // 8)]
    inverse = jnp.concatenate(inverse_factor(tiles, rows, lanes), axis=0)
    out_ref[whole : whole + width, :] = jnp.concatenate(split2(inverse), axis=1)


def first_tile(lengths, mine, sib):
    width = mine.shape[1]
    whole = 2 * (mine.shape[0] - 64)
    return pl.pallas_call(
        first_kernel,
        out_shape=jax.ShapeDtypeStruct((whole + width + 16, 2 * width), jnp.bfloat16),
        in_specs=[VM] * 3,
        out_specs=VM,
        scratch_shapes=[pltpu.VMEM((width, width), jnp.float32)],
        name="first_tile",
    )(lengths, mine, sib)


def dense(refs, t, width, depth):
    left = LANES - depth
    lane = lax.broadcasted_iota(jnp.int32, (width, LANES), 1)
    blocks = []
    for g in range(0, 8, 4):
        if t < 3:
            parts = [ref[t * width : (t + 1) * width, :] for ref in refs[g : g + 4]]
            for b in range(3):
                moved = pltpu.roll(parts[3], depth - left * b, 1)
                blocks.append(jnp.where(lane < depth, parts[b], moved))
        else:
            for b in range(3):
                block = refs[g + 3][b * width : (b + 1) * width, :]
                for k in range(3):
                    moved = pltpu.roll(
                        refs[g + b][k * width : (k + 1) * width, :], LANES - depth + left * k, 1
                    )
                    block = jnp.where((lane >= left * k) & (lane < left * (k + 1)), moved, block)
                blocks.append(block)
    return jnp.concatenate(blocks, axis=1)


def dense_weights(length_ref, depth):
    parts = dense_rows(jnp.concatenate(slice_weights(length_ref, depth), axis=0), depth)
    return jnp.broadcast_to(parts, (8 * depth, LANES)).T[0:1, :]


def three(x):
    hi, lo = split2(x)
    return jnp.concatenate([hi, lo, hi], axis=1)


def twice(y):
    hi, lo = split2(y)
    return jnp.concatenate([hi, hi, lo], axis=1)


def rest_kernel(depth, length_ref, noise_ref, first_hbm, *refs):
    row_refs, col_refs, (panel_hbm, trail_hbm, first_ref, panel_ref, trail_ref, sems) = refs[:4], refs[4:8], refs[8:]
    width, whole = noise_ref.shape[1], 8 * depth
    copy = pltpu.make_async_copy(first_hbm, first_ref, sems.at[0])
    copy.start()
    h = 3 * width
    cut = lambda ref, k: ref.at[pl.ds(k * h, h)]
    cuts = lambda ref: [ref.at[pl.ds(k * h, h)] for k in range(ref.shape[0] // h)]
    row_own, row_oth = cuts(row_refs[0]) + cuts(row_refs[1]), cuts(row_refs[2]) + cuts(row_refs[3])
    cols = sum((cuts(ref) for ref in col_refs), [])
    row_id, col_id, n_rows = lax.axis_index("row"), lax.axis_index("col"), lax.axis_size("row")
    parity, on_diag = col_id // n_rows, row_id == col_id % n_rows

    w = dense_weights(length_ref, depth)
    blocks = w.shape[1] // LANES

    def squares(xf, xw):
        partial = xf[:, 0:LANES] * xw[:, 0:LANES]
        for s in range(1, blocks):
            cut = slice(s * LANES, (s + 1) * LANES)
            partial = partial + xf[:, cut] * xw[:, cut]
        return partial

    eye = lax.broadcasted_iota(jnp.int32, (width, width), 0) == lax.broadcasted_iota(
        jnp.int32, (width, width), 1
    )
    copy.wait()
    inv = first_ref[whole : whole + width, :]
    inv = jnp.concatenate([inv[:, 0:width], inv], axis=1)
    tail = first_ref[whole + width :, :].astype(jnp.float32)
    tail = tail[0:1, :] + tail[1:2, :] + tail[2:3, :]
    sq0, diag0 = tail[:, 0:width], jnp.where(eye, tail[:, width:], 0.0)

    def kern_of(x, sq, heads):
        gram = jnp.dot(x, first_ref[0:whole, :], preferred_element_type=jnp.float32)
        gram = gram[:, 0:width] + gram[:, width:]
        kern = jnp.exp(gram - 0.5 * (sq + sq0))
        if heads:
            tops = [
                kern[h * width : (h + 1) * width] + jnp.where(c, diag0, 0.0)
                for h, c in enumerate(heads)
            ]
            if len(heads) * width < kern.shape[0]:
                tops.append(kern[len(heads) * width :])
            kern = jnp.concatenate(tops, axis=0)
        return kern

    c_hi, c_lo, c_sq, c_panel = [], [], [], []
    for t in range(4):
        c = dense(cols, t, width, depth)
        cf = c.astype(jnp.float32)
        cw = cf * w
        partial = squares(cf, cw)
        hi, lo = split2(cw)
        c_hi.append(hi)
        c_lo.append(lo)
        c_sq.append(jnp.sum(partial.T, axis=0, keepdims=True))
        sq = jnp.sum(partial, axis=1, keepdims=True)
        c_panel.append(kern_of(c, sq, [col_id == 0] if t == 0 else []))
    c_hi, c_lo = jnp.concatenate(c_hi, axis=0), jnp.concatenate(c_lo, axis=0)
    c_sq = jnp.concatenate(c_sq, axis=1)
    c_panel = twice(nt(three(jnp.concatenate(c_panel, axis=0)), inv))

    outs, xs, sqs, kerns = [], [], [], []
    for t in range(4):
        x = jnp.concatenate([dense(row_own, t, width, depth), dense(row_oth, t, width, depth)], axis=0)
        xf = x.astype(jnp.float32)
        sq = jnp.sum(squares(xf, xf * w), axis=1, keepdims=True)
        heads = [(row_id == 0) & (parity == h) for h in range(2)] if t == 0 else []
        xs.append(x)
        sqs.append(sq)
        kerns.append(kern_of(x, sq, heads))
    parts = []
    for t in range(4):
        panel = nt(three(kerns[t]), inv)
        parts.append(three(panel))
        for half in range(2):
            tile = 2 * t + (parity if half == 0 else 1 - parity)
            panel_ref[tile] = panel[half * width : (half + 1) * width]
            outs.append(pltpu.make_async_copy(panel_ref.at[tile], panel_hbm.at[tile], sems.at[1 + 2 * t + half]))
            outs[-1].start()
    for t in range(4):
        gram = nt(xs[t], c_hi) + nt(xs[t], c_lo)
        update = nt(parts[t], c_panel)
        trail = jnp.exp(gram - 0.5 * (sqs[t] + c_sq)) - update
        for half in range(2):
            tile = 2 * t + (parity if half == 0 else 1 - parity)
            low = half * width
            for tc in range(4):
                block = trail[low : low + width, tc * width : (tc + 1) * width]
                if half == 0 and tc == t:
                    block = block + jnp.where(eye & on_diag, noise_ref[pl.ds(tile, 1), :], 0.0)
                trail_ref[pl.ds(tile * (4 * width) + tc, width, stride=4), :] = block
            span = pl.ds(tile * (4 * width), 4 * width)
            outs.append(pltpu.make_async_copy(trail_ref.at[span], trail_hbm.at[span], sems.at[9 + 2 * t + half]))
            outs[-1].start()
    for copy in outs:
        copy.wait()


def rest(depth, lengths, noise, first, *slices):
    tiles, width = noise.shape
    return pl.pallas_call(
        functools.partial(rest_kernel, depth),
        out_shape=(
            jax.ShapeDtypeStruct((tiles, width, width), jnp.float32),
            jax.ShapeDtypeStruct((tiles * width * 4, width), jnp.float32),
        ),
        in_specs=[VM] * 2 + [ANY] + [VM] * 8,
        out_specs=(ANY, ANY),
        scratch_shapes=[
            pltpu.VMEM(first.shape, first.dtype),
            pltpu.VMEM((tiles, width, width), jnp.float32),
            pltpu.VMEM((tiles * width * 4 + 8, width), jnp.float32),
            pltpu.SemaphoreType.DMA((17,)),
        ],
        compiler_params=pltpu.CompilerParams(vmem_limit_bytes=VMEM_REST * 1024 * 1024),
        name="rest",
    )(lengths, noise, first, *slices)


def body(features, lengthscale, noise):
    tiles, width, depth = features.shape
    row_id = lax.axis_index("row")
    col_id = lax.axis_index("col")
    n_rows, n_cols = lax.axis_size("row"), lax.axis_size("col")
    home = col_id % n_rows
    parity = col_id // n_rows

    def over_row(x, k):
        return lax.ppermute(x, "row", [(i, i ^ k) for i in range(n_rows)])

    def over_col(x, k):
        return lax.ppermute(x, "col", [(i, i ^ k) for i in range(n_cols)])

    feats = jnp.transpose(features, (0, 2, 1))
    lengths = lengthscale.reshape(-1, LANES)

    def after(x, *others):
        return lax.optimization_barrier((x, *others))[0]

    own, oth, own_long, oth_long = pack(feats, noise)
    size = own.shape[0]
    near, p2, p3 = over_col(own, 2), over_col(oth, 4), over_col(oth, 6)
    first_planes = [own_long] + [over_row(own_long, k) for k in (1, 2, 3)]
    head = lax.select_n(row_id, *[v[size:] for v in first_planes])
    q1 = over_col(lax.dynamic_update_slice(oth_long, head, (size, 0)), 2)
    half = lax.dynamic_update_slice(own_long, head, (size, 0))
    q2, q3 = over_col(half, 4), over_col(half, 6)
    p = jnp.concatenate([near, p2, p3], axis=0)
    planes = [p] + [over_row(p, k) for k in (1, 2, 3)]
    p = jnp.concatenate([own, near, p2, p3], axis=0)
    stack = jnp.concatenate([head] + [v[size:] for v in (q1, q2, q3)], axis=0)
    first = first_tile(lengths, stack, over_col(stack, 1))
    q = jnp.concatenate([oth] + [v[:size] for v in (q1, q2, q3)], axis=0)
    sibs = [over_col(v, 1) for v in (p, q)]
    *planes, _ = lax.optimization_barrier((*planes, first))
    first_planes = [v[:size] for v in first_planes]
    keep = [lax.select_n(row_id ^ home, *v) for v in (first_planes, planes)]
    give = [over_col(lax.select_n(row_id ^ home ^ 1, *v), 1) for v in (first_planes, planes)]
    panel, trailing = rest(depth, lengths, noise, first, p, sibs[0], q, sibs[1], *keep, *give)
    return panel, trailing.reshape(tiles, width, 4, width)


def from_root(block, axis, holder):
    block = jnp.where(lax.axis_index(axis) == holder, block, jnp.zeros_like(block))
    return lax.psum(block, axis)


def general_body(features, lengthscale, noise):
    rows_axis = lax.axis_size("row")
    cols_axis = lax.axis_size("col")
    row_id = lax.axis_index("row")
    col_id = lax.axis_index("col")
    tiles_row = features.shape[0]
    width = features.shape[1]
    stride = cols_axis // rows_axis
    tiles_col = tiles_row // stride
    row_feats = lax.all_gather(features, "col", axis=2, tiled=True)
    depth = row_feats.shape[2]
    grouped = row_feats.reshape(tiles_col, stride, width, depth)
    picked = lax.dynamic_index_in_dim(grouped, col_id // rows_axis, 1, keepdims=False)
    col_feats = from_root(picked, "row", col_id % rows_axis)
    inverse = 1.0 / lengthscale
    left = row_feats.reshape(tiles_row * width, depth).astype(jnp.float32) * inverse[None, :]
    right = col_feats.reshape(tiles_col * width, depth).astype(jnp.float32) * inverse[None, :]
    left_sq = jnp.sum(left * left, axis=1)
    right_sq = jnp.sum(right * right, axis=1)
    inner = jnp.arange(width, dtype=jnp.int32)
    row_index = (
        (jnp.arange(tiles_row, dtype=jnp.int32)[:, None] * rows_axis + row_id) * width + inner[None, :]
    ).reshape(-1)
    col_index = (
        (jnp.arange(tiles_col, dtype=jnp.int32)[:, None] * cols_axis + col_id) * width + inner[None, :]
    ).reshape(-1)
    gram = jnp.dot(left, right.T, precision=lax.Precision.HIGHEST)
    kern = jnp.exp(-0.5 * (left_sq[:, None] + right_sq[None, :] - 2.0 * gram))
    kern = kern + jnp.where(row_index[:, None] == col_index[None, :], noise.reshape(-1)[:, None], 0.0)
    diag_tile = from_root(kern[:width, :width], "row", 0)
    factor = jnp.linalg.cholesky(diag_tile)
    own_rows = jax.scipy.linalg.solve_triangular(factor, kern[:, :width].T, lower=True).T
    panel_rows = from_root(own_rows, "col", 0)
    panel_grouped = panel_rows.reshape(tiles_col, stride, width, width)
    panel_pick = lax.dynamic_index_in_dim(panel_grouped, col_id // rows_axis, 1, keepdims=False)
    panel_cols = from_root(panel_pick, "row", col_id % rows_axis).reshape(tiles_col * width, width)
    trailing = kern - jnp.dot(panel_rows, panel_cols.T, precision=lax.Precision.HIGHEST)
    return (
        panel_rows.reshape(tiles_row, width, width),
        trailing.reshape(tiles_row, width, tiles_col, width),
    )


def solution(mesh):
    placed = (P(None, "row", "col"), P(), P(None, "row"))
    small = mesh.shape["row"] == 4 and mesh.shape["col"] == 8
    return jax.shard_map(
        body if small else general_body,
        mesh=mesh,
        in_specs=placed,
        out_specs=(P(None, "row", None), P(None, "row", None, "col")),
        check_vma=False,
    )
```

```python
import functools

import jax
import jax.numpy as jnp
from jax import lax
from jax.experimental import pallas as pl
from jax.experimental.pallas import tpu as pltpu
from jax.sharding import PartitionSpec as P

LANES = 128
VMEM_REST = 32
ORDER = (0, 2, 4, 6, 1, 3, 5, 7)
VM = pl.BlockSpec(memory_space=pltpu.VMEM)
ANY = pl.BlockSpec(memory_space=pl.ANY)


def nt(a, b, precision=None):
    return lax.dot_general(
        a, b, (((1,), (1,)), ((), ())), precision=precision, preferred_element_type=jnp.float32
    )


def split2(x):
    hi = x.astype(jnp.bfloat16)
    return hi, (x - hi.astype(jnp.float32)).astype(jnp.bfloat16)


def split3(x):
    hi, mid = split2(x)
    rest = x - hi.astype(jnp.float32) - mid.astype(jnp.float32)
    return hi, mid, rest.astype(jnp.bfloat16)


def pack_kernel(feat_ref, noise_ref, own_ref, oth_ref, own_long_ref, oth_long_ref):
    tiles, depth, width = feat_ref.shape
    left = LANES - depth
    parity = lax.axis_index("col") // lax.axis_size("row")
    for half, outs in ((0, (own_ref, own_long_ref)), (1, (oth_ref, oth_long_ref))):
        tile = [feat_ref[2 * k + (parity if half == 0 else 1 - parity)] for k in range(4)]
        for k in range(3):
            block = jnp.concatenate([tile[k], tile[3][left * k : left * (k + 1)]], axis=0).T
            for out_ref in outs:
                out_ref[k * width : (k + 1) * width, :] = block
    row = lax.broadcasted_iota(jnp.int32, (16, width), 0)
    parts = jnp.zeros((16, width), jnp.float32)
    for k, part in enumerate(split3(noise_ref[0:1, :])):
        parts = jnp.where(row == k, part.astype(jnp.float32), parts)
    for out_ref in (own_long_ref, oth_long_ref):
        out_ref[3 * width : 3 * width + depth, :] = feat_ref[0]
        out_ref[3 * width + depth :, :] = parts.astype(jnp.bfloat16)


def pack(feats, noise):
    _, depth, width = feats.shape
    rows = lambda n: jax.ShapeDtypeStruct((n, width), jnp.bfloat16)
    return pl.pallas_call(
        pack_kernel,
        out_shape=(
            rows(3 * width),
            rows(3 * width),
            rows(3 * width + depth + 16),
            rows(3 * width + depth + 16),
        ),
        in_specs=[VM, VM],
        out_specs=(VM,) * 4,
        name="pack",
    )(feats, noise)


def slice_weights(length_ref, depth):
    col_id = lax.axis_index("col")
    lane = lax.broadcasted_iota(jnp.int32, (8, LANES), 1)
    row = lax.broadcasted_iota(jnp.int32, (8, LANES), 0)
    held = jnp.ones((8, LANES), jnp.float32)
    for s in range(8):
        chunk, off = divmod(depth * s, LANES)
        here = jnp.broadcast_to(length_ref[chunk : chunk + 1, :], (8, LANES))
        if off:
            here = pltpu.roll(here, LANES - off, 1)
        if off + depth > LANES:
            more = jnp.broadcast_to(length_ref[chunk + 1 : chunk + 2, :], (8, LANES))
            here = jnp.where(lane < LANES - off, here, pltpu.roll(more, LANES - off, 1))
        for place, k in enumerate(ORDER):
            held = jnp.where((row == place) & (col_id == (s ^ k)), here, held)
    inverse = 1.0 / held
    columns = (inverse * inverse).T
    return [columns[0:depth, s : s + 1] for s in range(8)]


def bcast(v):
    return jnp.broadcast_to(v, (8, LANES))


def inverse_factor(tiles, rows, lanes, m=8, g=4):
    size = 8 * len(tiles)
    tiles, out = list(tiles), [None] * len(tiles)

    def total(terms):
        while len(terms) > 1:
            terms = [sum(terms[z : z + 2]) for z in range(0, len(terms), 2)]
        return terms[0]

    for k in range(0, size, m):
        b, j = divmod(k, 8)
        r = [bcast(tiles[b][j + i : j + i + 1, :]) for i in range(m)]
        s = [[bcast(r[i][:, k + l : k + l + 1]) if l >= i else None for l in range(m)] for i in range(m)]
        r = [r[i] + jnp.where(lanes == k + i, 1.0, 0.0) for i in range(m)]
        inv = [None] * m
        for q in range(0, m, g):
            scale, roots = None, []
            for p in range(q, q + g):
                product = s[p][p] if scale is None else scale * s[p][p]
                root = lax.rsqrt(product)
                inv[p] = root if scale is None else root * scale
                roots.append(root)
                for i in range(p + 1, q + g):
                    for l in range(m - 1, i - 1, -1):
                        s[i][l] = s[p][p] * s[i][l] - s[p][i] * s[p][l]
                    r[i] = s[p][p] * r[i] - s[p][i] * r[p]
                scale = product
            for p in range(q, q + g):
                r[p] = r[p] * roots[p - q]
                for l in range(p + 1, m):
                    s[p][l] = s[p][l] * roots[p - q]
            for i in range(q + g, m):
                for l in range(i, m):
                    s[i][l] = s[i][l] - total([s[p][i] * s[p][l] for p in range(q, q + g)])
                r[i] = r[i] - total([s[p][i] * r[p] for p in range(q, q + g)])
        for i in range(m):
            w = jnp.where(lanes < k + i, r[i], jnp.where(lanes == k + i, inv[i], 0.0))
            out[b] = w if out[b] is None else jnp.where(rows == j + i, w, out[b])
        if k + m >= size:
            break
        y = [r[i] * inv[i] for i in range(m)]
        for i in range(m):
            for l in range(i + 1, m):
                s[i][l] = s[i][l] * inv[i]
        for l in range(m - 1, 0, -1):
            for i in range(l - 1, -1, -1):
                y[i] = y[i] - s[i][l] * y[l]
        for i in range(b, len(tiles)):
            if i == b and j + m >= 8:
                continue
            terms = []
            for q in range(m):
                c = bcast(tiles[i][:, k + q : k + q + 1])
                if i == b:
                    c = jnp.where(rows > j + m - 1, c, 0.0)
                terms.append(c * y[q])
            tiles[i] = tiles[i] - total(terms)
    return out


def dense_rows(x, depth):
    left = LANES - depth
    blocks = []
    for g in range(0, 8, 4):
        for b in range(3):
            blocks.append(x[(g + b) * depth : (g + b + 1) * depth])
            last = (g + 3) * depth + left * b
            blocks.append(x[last : last + left])
    return jnp.concatenate(blocks, axis=0)


def first_kernel(length_ref, mine_hbm, sib_hbm, out_ref, work, mine_ref, sib_ref, sems):
    copies = [
        pltpu.make_async_copy(mine_hbm, mine_ref, sems.at[0]),
        pltpu.make_async_copy(sib_hbm, sib_ref, sems.at[1]),
    ]
    for copy in copies:
        copy.start()
    width = work.shape[0]
    each = mine_ref.shape[0] // 4
    depth = each - 16
    starts = range(0, 4 * each, each)
    w = jnp.concatenate(slice_weights(length_ref, depth), axis=0)
    for copy in copies:
        copy.wait()
    x = jnp.concatenate([ref[k : k + depth, :] for ref in (mine_ref, sib_ref) for k in starts], axis=0)
    xf = x.astype(jnp.float32)
    xw = xf * w
    parts = split3(xw)
    whole = 8 * depth
    out_ref[0:whole, :] = dense_rows(jnp.concatenate(parts[:2], axis=1), depth)
    turned = x.T
    gram = sum(jnp.dot(turned, part, preferred_element_type=jnp.float32) for part in parts)
    sq_row = jnp.sum(xf * xw, axis=0, keepdims=True)
    sq_col = jnp.broadcast_to(sq_row, (8, width)).T[:, 0:1]
    tail = mine_ref[depth:each, :].astype(jnp.float32)
    noise = tail[0:1, :] + tail[1:2, :] + tail[2:3, :]
    i = lax.broadcasted_iota(jnp.int32, (width, width), 0)
    j = lax.broadcasted_iota(jnp.int32, (width, width), 1)
    work[...] = jnp.exp(-0.5 * (sq_col + sq_row - 2.0 * gram)) + jnp.where(i == j, noise, 0.0)
    both = jnp.concatenate([sq_row, noise], axis=1)
    row = lax.broadcasted_iota(jnp.int32, (16, 2 * width), 0)
    rest = jnp.zeros((16, 2 * width), jnp.float32)
    for k, part in enumerate(split3(both)):
        rest = jnp.where(row == k, part.astype(jnp.float32), rest)
    out_ref[whole + width :, :] = rest.astype(jnp.bfloat16)
    rows = lax.broadcasted_iota(jnp.int32, (8, LANES), 0)
    lanes = lax.broadcasted_iota(jnp.int32, (8, LANES), 1)
    tiles = [work[8 * t : 8 * t + 8, :] for t in range(width // 8)]
    inverse = jnp.concatenate(inverse_factor(tiles, rows, lanes), axis=0)
    out_ref[whole : whole + width, :] = jnp.concatenate(split2(inverse), axis=1)


def first_tile(lengths, mine, sib):
    width = mine.shape[1]
    whole = 2 * (mine.shape[0] - 64)
    return pl.pallas_call(
        first_kernel,
        out_shape=jax.ShapeDtypeStruct((whole + width + 16, 2 * width), jnp.bfloat16),
        in_specs=[VM] + [ANY] * 2,
        out_specs=VM,
        scratch_shapes=[
            pltpu.VMEM((width, width), jnp.float32),
            pltpu.VMEM(mine.shape, mine.dtype),
            pltpu.VMEM(sib.shape, sib.dtype),
            pltpu.SemaphoreType.DMA((2,)),
        ],
        name="first_tile",
    )(lengths, mine, sib)


def dense(refs, t, width, depth):
    left = LANES - depth
    lane = lax.broadcasted_iota(jnp.int32, (width, LANES), 1)
    blocks = []
    for g in range(0, 8, 4):
        if t < 3:
            parts = [ref[t * width : (t + 1) * width, :] for ref in refs[g : g + 4]]
            for b in range(3):
                moved = pltpu.roll(parts[3], depth - left * b, 1)
                blocks.append(jnp.where(lane < depth, parts[b], moved))
        else:
            for b in range(3):
                block = refs[g + 3][b * width : (b + 1) * width, :]
                for k in range(3):
                    moved = pltpu.roll(
                        refs[g + b][k * width : (k + 1) * width, :], LANES - depth + left * k, 1
                    )
                    block = jnp.where((lane >= left * k) & (lane < left * (k + 1)), moved, block)
                blocks.append(block)
    return jnp.concatenate(blocks, axis=1)


def dense_weights(length_ref, depth):
    parts = dense_rows(jnp.concatenate(slice_weights(length_ref, depth), axis=0), depth)
    return jnp.broadcast_to(parts, (8 * depth, LANES)).T[0:1, :]


def three(x):
    hi, lo = split2(x)
    return jnp.concatenate([hi, lo, hi], axis=1)


def twice(y):
    hi, lo = split2(y)
    return jnp.concatenate([hi, hi, lo], axis=1)


def rest_kernel(depth, length_ref, noise_ref, first_hbm, *refs):
    row_refs, col_refs, (panel_hbm, trail_hbm, first_ref, panel_ref, trail_ref, sems) = refs[:4], refs[4:8], refs[8:]
    width, whole = noise_ref.shape[1], 8 * depth
    copy = pltpu.make_async_copy(first_hbm, first_ref, sems.at[0])
    copy.start()
    h = 3 * width
    cut = lambda ref, k: ref.at[pl.ds(k * h, h)]
    cuts = lambda ref: [ref.at[pl.ds(k * h, h)] for k in range(ref.shape[0] // h)]
    row_own, row_oth = cuts(row_refs[0]) + cuts(row_refs[1]), cuts(row_refs[2]) + cuts(row_refs[3])
    cols = sum((cuts(ref) for ref in col_refs), [])
    row_id, col_id, n_rows = lax.axis_index("row"), lax.axis_index("col"), lax.axis_size("row")
    parity, on_diag = col_id // n_rows, row_id == col_id % n_rows

    w = dense_weights(length_ref, depth)
    blocks = w.shape[1] // LANES

    def squares(xf, xw):
        partial = xf[:, 0:LANES] * xw[:, 0:LANES]
        for s in range(1, blocks):
            cut = slice(s * LANES, (s + 1) * LANES)
            partial = partial + xf[:, cut] * xw[:, cut]
        return partial

    eye = lax.broadcasted_iota(jnp.int32, (width, width), 0) == lax.broadcasted_iota(
        jnp.int32, (width, width), 1
    )
    copy.wait()
    inv = first_ref[whole : whole + width, :]
    inv = jnp.concatenate([inv[:, 0:width], inv], axis=1)
    tail = first_ref[whole + width :, :].astype(jnp.float32)
    tail = tail[0:1, :] + tail[1:2, :] + tail[2:3, :]
    sq0, diag0 = tail[:, 0:width], jnp.where(eye, tail[:, width:], 0.0)

    def kern_of(x, sq, heads):
        gram = jnp.dot(x, first_ref[0:whole, :], preferred_element_type=jnp.float32)
        gram = gram[:, 0:width] + gram[:, width:]
        kern = jnp.exp(gram - 0.5 * (sq + sq0))
        if heads:
            tops = [
                kern[h * width : (h + 1) * width] + jnp.where(c, diag0, 0.0)
                for h, c in enumerate(heads)
            ]
            if len(heads) * width < kern.shape[0]:
                tops.append(kern[len(heads) * width :])
            kern = jnp.concatenate(tops, axis=0)
        return kern

    c_hi, c_lo, c_sq, c_panel = [], [], [], []
    for t in range(4):
        c = dense(cols, t, width, depth)
        cf = c.astype(jnp.float32)
        cw = cf * w
        partial = squares(cf, cw)
        hi, lo = split2(cw)
        c_hi.append(hi)
        c_lo.append(lo)
        c_sq.append(jnp.sum(partial.T, axis=0, keepdims=True))
        sq = jnp.sum(partial, axis=1, keepdims=True)
        c_panel.append(kern_of(c, sq, [col_id == 0] if t == 0 else []))
    c_hi, c_lo = jnp.concatenate(c_hi, axis=0), jnp.concatenate(c_lo, axis=0)
    c_sq = jnp.concatenate(c_sq, axis=1)
    c_panel = twice(nt(three(jnp.concatenate(c_panel, axis=0)), inv))

    outs, xs, sqs, kerns = [], [], [], []
    for t in range(4):
        x = jnp.concatenate([dense(row_own, t, width, depth), dense(row_oth, t, width, depth)], axis=0)
        xf = x.astype(jnp.float32)
        sq = jnp.sum(squares(xf, xf * w), axis=1, keepdims=True)
        heads = [(row_id == 0) & (parity == h) for h in range(2)] if t == 0 else []
        xs.append(x)
        sqs.append(sq)
        kerns.append(kern_of(x, sq, heads))
    parts = []
    for t in range(4):
        panel = nt(three(kerns[t]), inv)
        parts.append(three(panel))
        for half in range(2):
            tile = 2 * t + (parity if half == 0 else 1 - parity)
            panel_ref[tile] = panel[half * width : (half + 1) * width]
            outs.append(pltpu.make_async_copy(panel_ref.at[tile], panel_hbm.at[tile], sems.at[1 + 2 * t + half]))
            outs[-1].start()
    for t in range(4):
        gram = nt(xs[t], c_hi) + nt(xs[t], c_lo)
        update = nt(parts[t], c_panel)
        trail = jnp.exp(gram - 0.5 * (sqs[t] + c_sq)) - update
        for half in range(2):
            tile = 2 * t + (parity if half == 0 else 1 - parity)
            low = half * width
            for tc in range(4):
                block = trail[low : low + width, tc * width : (tc + 1) * width]
                if half == 0 and tc == t:
                    block = block + jnp.where(eye & on_diag, noise_ref[pl.ds(tile, 1), :], 0.0)
                trail_ref[pl.ds(tile * (4 * width) + tc, width, stride=4), :] = block
            span = pl.ds(tile * (4 * width), 4 * width)
            outs.append(pltpu.make_async_copy(trail_ref.at[span], trail_hbm.at[span], sems.at[9 + 2 * t + half]))
            outs[-1].start()
    for copy in outs:
        copy.wait()


def rest(depth, lengths, noise, first, *slices):
    tiles, width = noise.shape
    return pl.pallas_call(
        functools.partial(rest_kernel, depth),
        out_shape=(
            jax.ShapeDtypeStruct((tiles, width, width), jnp.float32),
            jax.ShapeDtypeStruct((tiles * width * 4, width), jnp.float32),
        ),
        in_specs=[VM] * 2 + [ANY] + [VM] * 8,
        out_specs=(ANY, ANY),
        scratch_shapes=[
            pltpu.VMEM(first.shape, first.dtype),
            pltpu.VMEM((tiles, width, width), jnp.float32),
            pltpu.VMEM((tiles * width * 4 + 8, width), jnp.float32),
            pltpu.SemaphoreType.DMA((17,)),
        ],
        compiler_params=pltpu.CompilerParams(vmem_limit_bytes=VMEM_REST * 1024 * 1024),
        name="rest",
    )(lengths, noise, first, *slices)


def body(features, lengthscale, noise):
    tiles, width, depth = features.shape
    row_id = lax.axis_index("row")
    col_id = lax.axis_index("col")
    n_rows, n_cols = lax.axis_size("row"), lax.axis_size("col")
    home = col_id % n_rows
    parity = col_id // n_rows

    def over_row(x, k):
        return lax.ppermute(x, "row", [(i, i ^ k) for i in range(n_rows)])

    def over_col(x, k):
        return lax.ppermute(x, "col", [(i, i ^ k) for i in range(n_cols)])

    feats = jnp.transpose(features, (0, 2, 1))
    lengths = lengthscale.reshape(-1, LANES)

    def after(x, *others):
        return lax.optimization_barrier((x, *others))[0]

    own, oth, own_long, oth_long = pack(feats, noise)
    size = own.shape[0]
    near, p2, p3 = over_col(own, 2), over_col(oth, 4), over_col(oth, 6)
    first_planes = [own_long] + [over_row(own_long, k) for k in (1, 2, 3)]
    head = lax.select_n(row_id, *[v[size:] for v in first_planes])
    q1 = over_col(lax.dynamic_update_slice(oth_long, head, (size, 0)), 2)
    half = lax.dynamic_update_slice(own_long, head, (size, 0))
    q2, q3 = over_col(half, 4), over_col(half, 6)
    p = jnp.concatenate([near, p2, p3], axis=0)
    planes = [p] + [over_row(p, k) for k in (1, 2, 3)]
    p = jnp.concatenate([own, near, p2, p3], axis=0)
    stack = jnp.concatenate([head] + [v[size:] for v in (q1, q2, q3)], axis=0)
    first = first_tile(lengths, stack, over_col(stack, 1))
    q = jnp.concatenate([oth] + [v[:size] for v in (q1, q2, q3)], axis=0)
    sibs = [over_col(v, 1) for v in (p, q)]
    *planes, _ = lax.optimization_barrier((*planes, first))
    first_planes = [v[:size] for v in first_planes]
    keep = [lax.select_n(row_id ^ home, *v) for v in (first_planes, planes)]
    give = [over_col(lax.select_n(row_id ^ home ^ 1, *v), 1) for v in (first_planes, planes)]
    panel, trailing = rest(depth, lengths, noise, first, p, sibs[0], q, sibs[1], *keep, *give)
    return panel, trailing.reshape(tiles, width, 4, width)


def from_root(block, axis, holder):
    block = jnp.where(lax.axis_index(axis) == holder, block, jnp.zeros_like(block))
    return lax.psum(block, axis)


def general_body(features, lengthscale, noise):
    rows_axis = lax.axis_size("row")
    cols_axis = lax.axis_size("col")
    row_id = lax.axis_index("row")
    col_id = lax.axis_index("col")
    tiles_row = features.shape[0]
    width = features.shape[1]
    stride = cols_axis // rows_axis
    tiles_col = tiles_row // stride
    row_feats = lax.all_gather(features, "col", axis=2, tiled=True)
    depth = row_feats.shape[2]
    grouped = row_feats.reshape(tiles_col, stride, width, depth)
    picked = lax.dynamic_index_in_dim(grouped, col_id // rows_axis, 1, keepdims=False)
    col_feats = from_root(picked, "row", col_id % rows_axis)
    inverse = 1.0 / lengthscale
    left = row_feats.reshape(tiles_row * width, depth).astype(jnp.float32) * inverse[None, :]
    right = col_feats.reshape(tiles_col * width, depth).astype(jnp.float32) * inverse[None, :]
    left_sq = jnp.sum(left * left, axis=1)
    right_sq = jnp.sum(right * right, axis=1)
    inner = jnp.arange(width, dtype=jnp.int32)
    row_index = (
        (jnp.arange(tiles_row, dtype=jnp.int32)[:, None] * rows_axis + row_id) * width + inner[None, :]
    ).reshape(-1)
    col_index = (
        (jnp.arange(tiles_col, dtype=jnp.int32)[:, None] * cols_axis + col_id) * width + inner[None, :]
    ).reshape(-1)
    gram = jnp.dot(left, right.T, precision=lax.Precision.HIGHEST)
    kern = jnp.exp(-0.5 * (left_sq[:, None] + right_sq[None, :] - 2.0 * gram))
    kern = kern + jnp.where(row_index[:, None] == col_index[None, :], noise.reshape(-1)[:, None], 0.0)
    diag_tile = from_root(kern[:width, :width], "row", 0)
    factor = jnp.linalg.cholesky(diag_tile)
    own_rows = jax.scipy.linalg.solve_triangular(factor, kern[:, :width].T, lower=True).T
    panel_rows = from_root(own_rows, "col", 0)
    panel_grouped = panel_rows.reshape(tiles_col, stride, width, width)
    panel_pick = lax.dynamic_index_in_dim(panel_grouped, col_id // rows_axis, 1, keepdims=False)
    panel_cols = from_root(panel_pick, "row", col_id % rows_axis).reshape(tiles_col * width, width)
    trailing = kern - jnp.dot(panel_rows, panel_cols.T, precision=lax.Precision.HIGHEST)
    return (
        panel_rows.reshape(tiles_row, width, width),
        trailing.reshape(tiles_row, width, tiles_col, width),
    )


def solution(mesh):
    placed = (P(None, "row", "col"), P(), P(None, "row"))
    small = mesh.shape["row"] == 4 and mesh.shape["col"] == 8
    return jax.shard_map(
        body if small else general_body,
        mesh=mesh,
        in_specs=placed,
        out_specs=(P(None, "row", None), P(None, "row", None, "col")),
        check_vma=False,
    )
```
